512 devices in a mesh: dp: 64 (over x_lo, z, core), fsdp: 8 (over y, x_hi).
Axes of the slice: x: 4 (x_hi: 2, x_lo: 2; x = x_hi * 2 + x_lo), y: 4, z: 16, core: 2. Of those that a mesh axis runs over, the one named last changes fastest.
Arguments:
- tokens: bfloat16 [65536, 1024], P('dp'), may hold values from -8 to 8
- teacher: bfloat16 [512, 6144], P('dp'), may hold values from -8 to 8
- norm_gain: float32 [1024], replicated, may hold values from 0.25 to 1.75
- w_in: bfloat16 [1024, 4096], P(None, 'fsdp'), may hold values from -0.1875 to 0.1875
- b_in: float32 [4096], P('fsdp'), may hold values from -3 to 3
- w_out: bfloat16 [1024, 4096], P(None, 'fsdp'), may hold values from -0.09375 to 0.09375
- b_out: float32 [1024], replicated, may hold values from -3 to 3
- final_gain: float32 [1024], replicated, may hold values from 0.25 to 1.75
Outputs:
- loss_value: float32 [], replicated
- grad_in: bfloat16 [1024, 4096], P('dp', 'fsdp')
- grad_out: bfloat16 [1024, 4096], P('dp', 'fsdp')
The draws below stay inside these ranges and needn't reach their ends.
All inputs are finite; a program needn't handle non-finite values.
Results may differ from the reference program's by a relative error of at most 0.008.
Values may be sent and summed in bfloat16 or wider, within the bound.
A program may use at most 64 MiB of HBM per device.

```python
import jax
import jax.numpy as jnp
from jax import lax

D = 1024
DT = 6144
H = 4096
P_SIZE = 128
BLOCK = 8
IMAGES = 512
TOKENS = 65536
N_DP = 64


def draw_tokens(key, part):
    image_key, noise_key = jax.random.split(jax.random.fold_in(key, 11))
    image_part = jax.random.normal(image_key, (IMAGES, 1, D), jnp.float32)
    noise_part = jax.random.normal(noise_key, (IMAGES, P_SIZE, D), jnp.float32)
    values = jnp.clip(image_part + noise_part, -8.0, 8.0)
    return values.reshape(TOKENS, D).astype(jnp.bfloat16)


def draw_teacher(key, part):
    common_key, noise_key = jax.random.split(jax.random.fold_in(key, 23))
    common = jax.random.normal(common_key, (1, DT), jnp.float32)
    position = (jnp.arange(IMAGES, dtype=jnp.float32) + 0.5) / IMAGES
    noise = jax.random.normal(noise_key, (IMAGES, DT), jnp.float32)
    strength = 0.9 * position
    values = jnp.clip(noise + strength[:, None] * common, -8.0, 8.0)
    return values.astype(jnp.bfloat16)


def block_scale(rng, shape, shards, smallest, high):
    factor_of = 1.0
    for dim, parts in shards:
        heights = jax.random.uniform(jax.random.fold_in(jax.random.fold_in(rng, 6), dim), (parts,), jnp.float32, smallest / len(shards), high / len(shards))
        factor_of = factor_of * jnp.repeat(jnp.exp(heights), shape[dim] // parts).reshape((-1,) + (1,) * (len(shape) - 1 - dim))
    return factor_of


def gaussian(key, extent, deviation, reach, cuts=(), kind=jnp.bfloat16):
    entries = deviation * jax.random.normal(key, extent, jnp.float32)
    if cuts:
        entries = entries * block_scale(key, extent, cuts, -0.22, 0.18)
    return jnp.clip(entries, -reach, reach).astype(kind)


def setup_inputs(seed: int = 0) -> dict:
    seeds = jax.random.split(jax.random.key(seed), 9)
    tokens = draw_tokens(jax.random.fold_in(seeds[8], 71), 0)
    teacher = draw_teacher(jax.random.fold_in(seeds[8], 71), 0)
    norm_gain = jnp.clip(1.0 + 0.15 * jax.random.normal(seeds[2], (D,), jnp.float32), 0.25, 1.75)
    w_in = gaussian(seeds[3], (D, H), D ** -0.5, 0.1875, ((1, 8),))
    b_in = gaussian(seeds[4], (H,), 0.5, 3.0, ((0, 8),), jnp.float32)
    w_out = gaussian(seeds[5], (D, H), H ** -0.5, 0.09375, ((1, 8),))
    b_out = gaussian(seeds[6], (D,), 0.5, 3.0, (), jnp.float32)
    final_gain = jnp.clip(1.0 + 0.15 * jax.random.normal(seeds[7], (D,), jnp.float32), 0.25, 1.75)
    return dict(tokens=tokens, teacher=teacher, norm_gain=norm_gain, w_in=w_in, b_in=b_in, w_out=w_out, b_out=b_out, final_gain=final_gain)


loss_scale = 4096.0

def gelu_tanh(values):
    inner = 0.7978845608 * (values + 0.044715 * values * values * values)
    return 0.5 * values * (1.0 + jnp.tanh(inner))

def gelu_slope(values):
    inner = 0.7978845608 * (values + 0.044715 * values * values * values)
    tangent = jnp.tanh(inner)
    return 0.5 * (1.0 + tangent) + 0.5 * values * (1.0 - tangent * tangent) * 0.7978845608 * (1.0 + 3.0 * 0.044715 * values * values)

def layer_norm(values, gain_vec):
    centered = values - lax.optimization_barrier(jnp.mean(values, axis=-1, keepdims=True))
    inv_std = lax.rsqrt(lax.optimization_barrier(jnp.mean(centered * centered, axis=-1, keepdims=True)) + 1e-05)
    normed = centered * inv_std
    return (normed * gain_vec, normed, inv_std)

def reference(tokens, teacher, norm_gain, w_in, b_in, w_out, b_out, final_gain):
    tok_blocks = tokens.reshape(N_DP, BLOCK * P_SIZE, D)

    def forward_block(tok_block):
        token_values = tok_block.astype(jnp.float32)
        normed_tokens = layer_norm(token_values, norm_gain)[0].astype(jnp.bfloat16)
        pre_act = jnp.dot(normed_tokens, w_in, preferred_element_type=jnp.float32) + b_in
        pooled = gelu_tanh(pre_act).reshape(BLOCK, P_SIZE, H).mean(axis=1).astype(jnp.bfloat16)
        token_mean = token_values.reshape(BLOCK, P_SIZE, D).mean(axis=1)
        return (pooled, token_mean)
    pooled, token_mean = lax.map(forward_block, tok_blocks)
    pooled = pooled.reshape(IMAGES, H)
    token_mean = token_mean.reshape(IMAGES, D)
    branch = lax.dot_general(pooled, w_out, (((1,), (1,)), ((), ())), preferred_element_type=jnp.float32)
    embedding = token_mean + branch + b_out
    scaled_unit, normed_embed, inv_std = layer_norm(embedding, final_gain)
    unit_norm = jnp.sqrt(lax.optimization_barrier(jnp.sum(scaled_unit * scaled_unit, axis=-1, keepdims=True)) + 1e-06)
    unit_dir = scaled_unit / unit_norm
    student = unit_dir.astype(jnp.bfloat16)
    teacher_f = teacher.astype(jnp.float32)
    target = (teacher_f / jnp.sqrt(lax.optimization_barrier(jnp.sum(teacher_f * teacher_f, axis=-1, keepdims=True)) + 1e-06)).astype(jnp.bfloat16)
    resid = jnp.dot(student, student.T, preferred_element_type=jnp.float32) - jnp.dot(target, target.T, preferred_element_type=jnp.float32)
    loss_value = jnp.sum(resid * resid) / IMAGES
    dstudent = loss_scale * 4.0 / IMAGES * jnp.dot(resid.astype(jnp.bfloat16), student, preferred_element_type=jnp.float32)
    dunit = (dstudent - unit_dir * lax.optimization_barrier(jnp.sum(unit_dir * dstudent, axis=-1, keepdims=True))) / unit_norm
    gain_grad = dunit * final_gain
    dembed = inv_std * (gain_grad - lax.optimization_barrier(jnp.mean(gain_grad, axis=-1, keepdims=True)) - normed_embed * lax.optimization_barrier(jnp.mean(gain_grad * normed_embed, axis=-1, keepdims=True)))
    dembed_b = dembed.astype(jnp.bfloat16)
    grad_out = lax.dot_general(dembed_b, pooled, (((0,), (0,)), ((), ())), preferred_element_type=jnp.float32).astype(jnp.bfloat16)
    dpooled = jnp.dot(dembed_b, w_out, preferred_element_type=jnp.float32)

    def grad_block(running, pieces):
        tok_block, dpool_block = pieces
        token_values = tok_block.astype(jnp.float32)
        normed_tokens = layer_norm(token_values, norm_gain)[0].astype(jnp.bfloat16)
        pre_act = jnp.dot(normed_tokens, w_in, preferred_element_type=jnp.float32) + b_in
        slope = gelu_slope(pre_act.reshape(BLOCK, P_SIZE, H))
        dhidden = (dpool_block[:, None, :] / P_SIZE * slope).reshape(BLOCK * P_SIZE, H).astype(jnp.bfloat16)
        term = lax.dot_general(normed_tokens, dhidden, (((0,), (0,)), ((), ())), preferred_element_type=jnp.float32)
        return (running + term, None)
    grad_in, _ = lax.scan(grad_block, jnp.zeros((D, H), jnp.float32), (tok_blocks, dpooled.reshape(N_DP, BLOCK, H)))
    return (loss_value, grad_in.astype(jnp.bfloat16), grad_out)
```

```python
import jax
import jax.numpy as jnp
from jax import lax
from jax.experimental import pallas as pl
from jax.experimental.pallas import tpu as pltpu
from jax.sharding import PartitionSpec as P

MESH = pl.DeviceIdType.MESH
F32 = jnp.float32
BF16 = jnp.bfloat16

NZ = 16
NF = 8
NP = 32
LOSS_SCALE = 4096.0
IMAGES = 512
PER_IMAGE = 128
D = 1024
DT = 6144
HID = 512


def dot(left, right):
    return jnp.dot(left, right, preferred_element_type=F32)


def dot_last(left, right):
    return lax.dot_general(left, right, (((1,), (1,)), ((), ())), preferred_element_type=F32)


def dot_first(left, right):
    return lax.dot_general(left, right, (((0,), (0,)), ((), ())), preferred_element_type=F32)


def dot_exact(values, ones):
    high = values.astype(BF16)
    rest = values - high.astype(F32)
    mid = rest.astype(BF16)
    low = (rest - mid.astype(F32)).astype(BF16)
    return dot(high, ones) + dot(mid, ones) + dot(low, ones)


def iota(shape, axis):
    return lax.broadcasted_iota(jnp.int32, shape, axis)


def gelu_parts(values):
    inner = 0.7978845608 * (values + 0.044715 * values * values * values)
    return jnp.tanh(inner)


def kernel(
    tok, tea, ng, win, b_in, wout, b_out, fg,
    loss_ref, gin_ref, gout_ref,
    normed, pre, slope, dhid, tmean, pooled_f, part64, tm64,
    tflat, tp, tj, trow, c1b, st_row, sp, sj, dref, da, dmsg, db,
    px, pin, pout16, pall, zmsg, dz,
    own, sib, coreb, xs, xb, totf, zs, zb,
    s_tq, r_tq, s_tz, r_tz, s_c1, r_c1, s_px, r_px, s_cz, r_cz, s_cp, r_cp,
    s_da, r_da, s_db, r_db, s_pz, r_pz, s_pc, r_pc, s_dz, r_dz,
    s_co, r_co, s_x, r_x, s_z, r_z,
):
    d = lax.axis_index("dp")
    f = lax.axis_index("fsdp")
    xl = d // (2 * NZ)
    z = (d // 2) % NZ
    c = d % 2
    q = xl * 2 + c
    p = q * NF + f

    def dev(xx, zz, cc, ff):
        return ((xx * NZ + zz) * 2 + cc, ff)

    def plane(k):
        qq = (q + k // NF) % 4
        ff = (f + k % NF) % NF
        return qq, ff, qq * NF + ff

    def copy(src, dst, ss, rs, to):
        return pltpu.make_async_remote_copy(
            src_ref=src, dst_ref=dst, send_sem=ss, recv_sem=rs, device_id=to, device_id_type=MESH
        )

    def each(lo, hi, fn):
        def step(k, carry):
            fn(k)
            return carry

        lax.fori_loop(lo, hi, step, 0)

    barrier = pltpu.get_barrier_semaphore()

    def sig_plane(k):
        qq, ff, _ = plane(k)
        pl.semaphore_signal(
            barrier, inc=1, device_id=dev(qq // 2, z, qq % 2, ff), device_id_type=MESH
        )

    def sig_z(k):
        pl.semaphore_signal(
            barrier, inc=1, device_id=dev(xl, (z + k) % NZ, c, f), device_id_type=MESH
        )

    each(1, NP, sig_plane)
    each(1, NZ, sig_z)

    teacher = tea[...].astype(F32)
    t_norm = jnp.sqrt(jnp.sum(teacher * teacher, axis=-1, keepdims=True) + 1e-06)
    target = teacher / t_norm
    for a in range(16):
        for b in range(3):
            lo = 384 * a + 128 * b
            tflat[b, pl.ds(a, 8, stride=16), :] = target[:, lo : lo + 128]
    tp[q] = jnp.concatenate([tflat[b] for b in range(3)], axis=1).astype(BF16)
    own_rows = pl.ds(pl.multiple_of(f * 16, 16), 16)
    own_target = jnp.concatenate([tflat[b, own_rows, :] for b in range(3)], axis=1).astype(BF16)
    trow[...] = own_target
    tj[z] = own_target

    pl.semaphore_wait(barrier, NP - 1 + NZ - 1)

    def tq_copy(k):
        qq = (q + k) % 4
        return copy(
            tp.at[q], tp.at[q], s_tq.at[k], r_tq.at[q], dev(qq // 2, z, qq % 2, f)
        )

    def tz_copy(k):
        return copy(trow, tj.at[z], s_tz.at[k], r_tz.at[z], dev(xl, (z + k) % NZ, c, f))

    each(1, NZ, lambda k: tz_copy(k).start())
    each(1, 4, lambda k: tq_copy(k).start())

    gain = ng[...]
    bias = b_in[...]

    def forward(i):
        rows = pl.ds(pl.multiple_of(i * 256, 256), 256)
        x = tok[rows, :].astype(F32)
        tmean[pl.ds(2 * i, 1), :] = jnp.sum(x[:128], axis=0, keepdims=True) * (1.0 / PER_IMAGE)
        tmean[pl.ds(2 * i + 1, 1), :] = jnp.sum(x[128:], axis=0, keepdims=True) * (1.0 / PER_IMAGE)
        centered = x - jnp.mean(x, axis=-1, keepdims=True)
        inv = lax.rsqrt(jnp.mean(centered * centered, axis=-1, keepdims=True) + 1e-05)
        nb = (centered * inv * gain).astype(BF16)
        normed[rows, :] = nb
        act = dot(nb, win[...]) + bias
        pre[rows, :] = act
        g = 0.5 * act * (1.0 + gelu_parts(act))
        pooled_f[pl.ds(2 * i, 1), :] = jnp.sum(g[:128], axis=0, keepdims=True) * (1.0 / PER_IMAGE)
        pooled_f[pl.ds(2 * i + 1, 1), :] = jnp.sum(g[128:], axis=0, keepdims=True) * (
            1.0 / PER_IMAGE
        )

    each(0, 4, forward)
    pooled_b = pooled_f[...].astype(BF16)
    partial = dot_last(pooled_b, wout[...])
    mean_tok = tmean[...]
    for a in range(8):
        part64[pl.ds(a, 8, stride=8), :] = partial[:, 128 * a : 128 * a + 128]
        tm64[pl.ds(a, 8, stride=8), :] = mean_tok[:, 128 * a : 128 * a + 128]

    def c1_copy(k):
        ff = (f + k) % NF
        return copy(
            part64.at[pl.ds(pl.multiple_of(ff * 8, 8), 8)],
            c1b.at[f], s_c1.at[k], r_c1.at[f], (d, ff),
        )

    each(1, NF, lambda k: c1_copy(k).start())
    c1b[f] = part64[pl.ds(pl.multiple_of(f * 8, 8), 8), :]
    px[...] = pooled_b.astype(F32)

    def px_copy():
        return copy(px, pin, s_px, r_px, dev(1 - xl, z, c, f))

    px_copy().start()

    def slopes(i):
        rows = pl.ds(pl.multiple_of(i * 128, 128), 128)
        v = pre[rows, :]
        t = gelu_parts(v)
        slope[rows, :] = 0.5 * (1.0 + t) + 0.5 * v * (1.0 - t * t) * 0.7978845608 * (
            1.0 + 3.0 * 0.044715 * v * v
        )

    each(0, 8, slopes)

    def wait_from(dst, ss, rs):
        copy(dst, dst, ss, rs, (d, f)).wait_recv()

    def c1_wait(k):
        ff = (f + k) % NF
        wait_from(c1b.at[ff], s_c1.at[k], r_c1.at[ff])

    each(1, NF, c1_wait)
    embedding = jnp.sum(c1b[...], axis=0) + tm64[pl.ds(pl.multiple_of(f * 8, 8), 8), :] + b_out[...]
    final_gain = fg[...]

    def total(v):
        return jnp.sum(jnp.sum(v, axis=1, keepdims=True), axis=0, keepdims=True)

    cent = embedding - total(embedding) * (1.0 / D)
    inv_std = lax.rsqrt(total(cent * cent) * (1.0 / D) + 1e-05)
    n_emb = cent * inv_std
    unit = n_emb * final_gain
    unit_norm = jnp.sqrt(total(unit * unit) + 1e-06)
    unit_dir = unit / unit_norm
    student = unit_dir.astype(BF16).astype(F32)
    st_row[...] = student

    def cz_copy(k):
        return copy(st_row, sj.at[z], s_cz.at[k], r_cz.at[z], dev(xl, (z + k) % NZ, c, f))

    def cp_copy(k):
        qq, ff, _ = plane(k)
        return copy(st_row, sp.at[p], s_cp.at[k], r_cp.at[p], dev(qq // 2, z, qq % 2, ff))

    each(1, NZ, lambda k: cz_copy(k).start())
    each(1, NP, lambda k: cp_copy(k).start())
    sj[z] = student
    sp[p] = student

    def tq_wait(k):
        qq = (q + k) % 4
        wait_from(tp.at[qq], s_tq.at[k], r_tq.at[qq])

    def tz_wait(k):
        zz = (z + k) % NZ
        wait_from(tj.at[zz], s_tz.at[k], r_tz.at[zz])

    each(1, 4, tq_wait)
    each(1, NZ, tz_wait)
    tx = dot_last(tp[...].reshape(NP * 16, 384), tj[...].reshape(NZ * 16, 384))
    same = (iota(tx.shape, 0) % 16) == (iota(tx.shape, 1) % 16)
    tx = jnp.sum(jnp.where(same, tx, 0.0).reshape(NP, 16, NZ * 16), axis=1)
    spread = ((iota((NZ * 16, 128), 0) // 16) == (iota((NZ * 16, 128), 1) // 8)).astype(BF16)
    gram_t = dot_exact(tx, spread)

    def pz_copy(k):
        return copy(
            pout16, pall.at[c, z], s_pz.at[k], r_pz.at[z], dev(xl, (z + k) % NZ, c, f)
        )

    wait_from(pin, s_px, r_px)
    mine, other = px[...], pin[...]
    first = xl == 0
    block16 = jnp.concatenate(
        [jnp.where(first, mine, other), jnp.where(first, other, mine)], axis=0
    ).astype(BF16)
    pout16[...] = block16
    pall[c, z] = block16

    def cz_wait(k):
        zz = (z + k) % NZ
        wait_from(sj.at[zz], s_cz.at[k], r_cz.at[zz])

    def cp_wait(k):
        _, _, pp = plane(k)
        wait_from(sp.at[pp], s_cp.at[k], r_cp.at[pp])

    each(1, NP, cp_wait)
    each(1, NZ, cz_wait)
    s_plane = sp[...].reshape(NP * 8, 128).astype(BF16)
    s_other = sj[...].reshape(NZ * 8, 128).astype(BF16)
    sx = dot_last(s_plane, s_other)
    diag = (iota(sx.shape, 0) % 8) == (iota(sx.shape, 1) % 8)
    sx = jnp.sum(jnp.where(diag, sx, 0.0).reshape(NP, 8, 128), axis=1)
    group = ((iota((128, 128), 0) // 8) == (iota((128, 128), 1) // 8)).astype(BF16)
    resid = dot_exact(sx, group) - gram_t
    share = total(resid * resid) * 0.125
    wide = jnp.broadcast_to(resid[:, None, :], (NP, 8, 128)).reshape(NP * 8, 128)
    wide = jnp.where(diag, wide, 0.0).astype(BF16)
    dref[...] = dot(wide, s_other).reshape(NP, 8, 128)

    def da_copy(k):
        qq, ff, pp = plane(k)
        return copy(dref.at[pp], da.at[p], s_da.at[k], r_da.at[p], dev(qq // 2, z, qq % 2, ff))

    each(1, NP, lambda k: da_copy(k).start())
    da[p] = dref[p]
    each(1, NZ, lambda k: pz_copy(k).start())

    def da_wait(k):
        _, _, pp = plane(k)
        wait_from(da.at[pp], s_da.at[k], r_da.at[pp])

    each(1, NP, da_wait)
    dstudent = (LOSS_SCALE * 4.0 / IMAGES) * jnp.sum(da[...], axis=0)
    dunit = (dstudent - unit_dir * total(unit_dir * dstudent)) / unit_norm
    gain_grad = dunit * final_gain
    dembed = inv_std * (
        gain_grad - total(gain_grad) * (1.0 / D) - n_emb * (total(gain_grad * n_emb) * (1.0 / D))
    )
    message = jnp.concatenate(
        [dembed.astype(BF16).astype(F32), jnp.broadcast_to(share, (8, 128))], axis=0
    )
    dmsg[...] = message

    def rows16(pp):
        return pl.ds(pl.multiple_of(pp * 16, 16), 16)

    def db_copy(k):
        qq, ff, _ = plane(k)
        return copy(
            dmsg, db.at[rows16(p)], s_db.at[k], r_db.at[p], dev(qq // 2, z, qq % 2, ff)
        )

    each(1, NP, lambda k: db_copy(k).start())
    db[rows16(p), :] = message

    def db_wait(k):
        _, _, pp = plane(k)
        wait_from(db.at[rows16(pp)], s_db.at[k], r_db.at[pp])

    each(1, NF, db_wait)
    block = jnp.concatenate(
        [db[pl.ds(q * (NF * 16) + a, 8, stride=16), :] for a in range(8)], axis=1
    ).astype(BF16)
    tmean[:, :HID] = dot(block, wout[...]) * (1.0 / PER_IMAGE)

    def hidden(i):
        rows = pl.ds(pl.multiple_of(i * PER_IMAGE, PER_IMAGE), PER_IMAGE)
        dhid[rows, :] = (tmean[pl.ds(i, 1), :HID] * slope[rows, :]).astype(BF16)

    each(0, 8, hidden)

    low = c == 0

    def co_copy(j):
        return copy(sib.at[j], coreb.at[j], s_co.at[j], r_co.at[j], dev(xl, z, 1 - c, f))

    def x_copy(j):
        return copy(xs.at[j], xb.at[j], s_x.at[j], r_x.at[j], dev(1 - xl, z, c, f))

    for j in range(4):
        side = (1 - xl) if j < 2 else xl
        cols = pl.ds(pl.multiple_of(side * 512 + (j % 2) * 256, 256), 256)
        term = dot_first(normed[:, cols], dhid[...]).reshape(8, 2, 16, HID)
        own[j] = jnp.where(low, term[:, 0], term[:, 1])
        sib[j] = jnp.where(low, term[:, 1], term[:, 0]).astype(BF16)
        co_copy(j).start()
        if j >= 1 and j <= 2:
            wait_from(coreb.at[j - 1], s_co.at[j - 1], r_co.at[j - 1])
            xs[j - 1] = (own[j - 1] + coreb[j - 1].astype(F32)).astype(BF16)
            x_copy(j - 1).start()

    each(NF, NP, db_wait)
    loss_plane = jnp.zeros((8, 128), F32)
    for pp in range(NP):
        loss_plane = loss_plane + db[pp * 16 + 8 : pp * 16 + 16, :]
    flat = jnp.concatenate(
        [db[pl.ds(xl * 4 + a, NP, stride=16), :] for a in range(4)], axis=1
    ).astype(BF16)
    image = iota((NP, 128), 0)
    lane = ((image // 8) % 2) * 64 + (z % 4) * 16 + (image // 16) * 8 + image % 8
    place = (lane == iota((NP, 128), 1)).astype(BF16)
    turned = dot_first(flat, place).reshape(NZ, 2, 16, 128)
    zmsg[:, 0:16, :] = jnp.where(low, turned[:, 0], turned[:, 1])
    zmsg[:, 16:24, :] = jnp.broadcast_to(loss_plane[None], (NZ, 8, 128))
    dz[z] = zmsg[z]

    def dz_copy(k):
        zz = (z + k) % NZ
        return copy(zmsg.at[zz], dz.at[z], s_dz.at[k], r_dz.at[z], dev(xl, zz, c, f))

    each(1, NZ, lambda k: dz_copy(k).start())

    def z_copy(zz):
        return copy(zs.at[zz], zb.at[z], s_z.at[zz], r_z.at[z], dev(xl, zz, c, f))

    zb[z] = jnp.zeros((16, HID), BF16)
    for h in range(2):
        j = 2 + h
        wait_from(coreb.at[j], s_co.at[j], r_co.at[j])
        wait_from(xb.at[h], s_x.at[h], r_x.at[h])
        merged = own[j] + coreb[j].astype(F32) + xb[h].astype(F32)
        totf[8 * h : 8 * h + 8] = merged
        zs[8 * h : 8 * h + 8] = merged.astype(BF16)

        def z_start(zz):
            @pl.when(zz != z)
            def _():
                z_copy(zz).start()

        each(8 * h, 8 * h + 8, z_start)

    def pz_wait(k):
        zz = (z + k) % NZ
        wait_from(pall.at[c, zz], s_pz.at[k], r_pz.at[zz])

    each(1, NZ, pz_wait)

    def pc_copy():
        return copy(pall.at[c], pall.at[c], s_pc, r_pc, dev(xl, z, 1 - c, f))

    pc_copy().start()

    def dz_wait(k):
        zz = (z + k) % NZ
        wait_from(dz.at[zz], s_dz.at[k], r_dz.at[zz])

    each(1, NZ, dz_wait)
    wait_from(pall.at[1 - c], s_pc, r_pc)
    acc = jnp.zeros((16, HID), F32)
    loss = jnp.zeros((8, 128), F32)
    for g in range(NZ // 4):
        left = jnp.zeros((16, 128), F32)
        for zz in range(4 * g, 4 * g + 4):
            left = left + dz[zz, 0:16, :]
            loss = loss + dz[zz, 16:24, :]
        right = jnp.concatenate(
            [pall[cc, 4 * g : 4 * g + 4].reshape(64, HID) for cc in range(2)], axis=0
        )
        acc = acc + dot(left.astype(BF16), right)
    gout_ref[...] = acc.astype(BF16)
    loss_ref[...] = loss * (1.0 / IMAGES)

    def z_wait(k):
        zz = (z + k) % NZ
        wait_from(zb.at[zz], s_z.at[zz], r_z.at[zz])

    each(1, NZ, z_wait)
    gin_ref[...] = (totf[z] + jnp.sum(zb[...].astype(F32), axis=0)).astype(BF16)

    each(1, 4, lambda k: tq_copy(k).wait_send())
    each(1, NZ, lambda k: tz_copy(k).wait_send())
    each(1, NF, lambda k: c1_copy(k).wait_send())
    px_copy().wait_send()
    each(1, NZ, lambda k: cz_copy(k).wait_send())
    each(1, NP, lambda k: cp_copy(k).wait_send())
    each(1, NP, lambda k: da_copy(k).wait_send())
    each(1, NZ, lambda k: pz_copy(k).wait_send())
    each(1, NP, lambda k: db_copy(k).wait_send())
    each(1, NZ, lambda k: dz_copy(k).wait_send())
    each(0, 4, lambda j: co_copy(j).wait_send())
    each(0, 2, lambda j: x_copy(j).wait_send())
    each(1, NZ, lambda k: z_copy((z + k) % NZ).wait_send())
    pc_copy().wait_send()


def body(tokens, teacher, norm_gain, w_in, b_in, w_out, b_out, final_gain):
    vmem = pl.BlockSpec(memory_space=pltpu.VMEM)
    sems = []
    for n in (4, NZ, NF, None, NZ, NP, NP, NP, NZ, None, NZ, 4, 2, NZ):
        sems += [pltpu.SemaphoreType.DMA if n is None else pltpu.SemaphoreType.DMA((n,))] * 2
    loss, grad_in, grad_out = pl.pallas_call(
        kernel,
        name="gram_step",
        out_shape=(
            jax.ShapeDtypeStruct((8, 128), F32),
            jax.ShapeDtypeStruct((16, HID), BF16),
            jax.ShapeDtypeStruct((16, HID), BF16),
        ),
        in_specs=[vmem] * 8,
        out_specs=(vmem, vmem, vmem),
        scratch_shapes=[
            pltpu.VMEM((1024, D), BF16),
            pltpu.VMEM((1024, HID), F32),
            pltpu.VMEM((1024, HID), F32),
            pltpu.VMEM((1024, HID), BF16),
            pltpu.VMEM((8, D), F32),
            pltpu.VMEM((8, HID), F32),
            pltpu.VMEM((64, 128), F32),
            pltpu.VMEM((64, 128), F32),
            pltpu.VMEM((3, 128, 128), F32),
            pltpu.VMEM((4, 128, 384), BF16),
            pltpu.VMEM((NZ, 16, 384), BF16),
            pltpu.VMEM((16, 384), BF16),
            pltpu.VMEM((NF, 8, 128), F32),
            pltpu.VMEM((8, 128), F32),
            pltpu.VMEM((NP, 8, 128), F32),
            pltpu.VMEM((NZ, 8, 128), F32),
            pltpu.VMEM((NP, 8, 128), F32),
            pltpu.VMEM((NP, 8, 128), F32),
            pltpu.VMEM((16, 128), F32),
            pltpu.VMEM((NP * 16, 128), F32),
            pltpu.VMEM((8, HID), F32),
            pltpu.VMEM((8, HID), F32),
            pltpu.VMEM((16, HID), BF16),
            pltpu.VMEM((2, NZ, 16, HID), BF16),
            pltpu.VMEM((NZ, 24, 128), F32),
            pltpu.VMEM((NZ, 24, 128), F32),
            pltpu.VMEM((4, 8, 16, HID), F32),
            pltpu.VMEM((4, 8, 16, HID), BF16),
            pltpu.VMEM((4, 8, 16, HID), BF16),
            pltpu.VMEM((2, 8, 16, HID), BF16),
            pltpu.VMEM((2, 8, 16, HID), BF16),
            pltpu.VMEM((NZ, 16, HID), F32),
            pltpu.VMEM((NZ, 16, HID), BF16),
            pltpu.VMEM((NZ, 16, HID), BF16),
        ]
        + sems,
        compiler_params=pltpu.CompilerParams(
            collective_id=0, has_side_effects=True, vmem_limit_bytes=48 << 20
        ),
        cost_estimate=pl.CostEstimate(
            flops=5_000_000_000, bytes_accessed=8_000_000, transcendentals=1_000_000
        ),
    )(
        tokens,
        teacher,
        norm_gain.reshape(1, D),
        w_in,
        b_in.reshape(1, HID),
        w_out,
        b_out.reshape(8, 128),
        final_gain.reshape(8, 128),
    )
    return loss[0, 0], grad_in, grad_out


def solution(mesh):
    return jax.shard_map(
        body,
        mesh=mesh,
        in_specs=(
            P("dp", None),
            P("dp", None),
            P(),
            P(None, "fsdp"),
            P("fsdp"),
            P(None, "fsdp"),
            P(),
            P(),
        ),
        out_specs=(P(), P("dp", "fsdp"), P("dp", "fsdp")),
        check_vma=False,
    )
```

```python
import jax
import jax.numpy as jnp
from jax import lax
from jax.experimental import pallas as pl
from jax.experimental.pallas import tpu as pltpu
from jax.sharding import PartitionSpec as P

MESH = pl.DeviceIdType.MESH
F32 = jnp.float32
BF16 = jnp.bfloat16

NZ = 16
NF = 8
NW = 8
NP = 32
LOSS_SCALE = 4096.0
IMAGES = 512
PER_IMAGE = 128
D = 1024
DT = 6144
HID = 512


def dot(left, right):
    return jnp.dot(left, right, preferred_element_type=F32)


def dot_last(left, right):
    return lax.dot_general(left, right, (((1,), (1,)), ((), ())), preferred_element_type=F32)


def dot_first(left, right):
    return lax.dot_general(left, right, (((0,), (0,)), ((), ())), preferred_element_type=F32)


def dot_exact(values, ones):
    high = values.astype(BF16)
    rest = values - high.astype(F32)
    mid = rest.astype(BF16)
    low = (rest - mid.astype(F32)).astype(BF16)
    return dot(high, ones) + dot(mid, ones) + dot(low, ones)


def div(value, by):
    return lax.div(value, jnp.int32(by))


def rem(value, by):
    return lax.rem(value, jnp.int32(by))


def iota(shape, axis):
    return lax.broadcasted_iota(jnp.int32, shape, axis)


def gelu_parts(values):
    inner = 0.7978845608 * (values + 0.044715 * values * values * values)
    return jnp.tanh(inner)


def kernel(
    tok_h, tea_h, ng_h, win_h, b_in_h, wout_h, b_out_h, fg_h,
    out_ref, loss_ref,
    tok, tea, ng, win, b_in, wout, b_out, fg, s_in,
    normed, pre, slope, dhid, tmean, pooled_f, part64, tm64,
    tflat, tp, tj, trow, c1b, st_row, sp, sj, dref, da, dmsg, db,
    px, pin, pout16, pall, zmsg, dz,
    own, sib, coreb, xs, xb, totf, zs, zb,
    s_tq, r_tq, s_tz, r_tz, s_c1, r_c1, s_px, r_px, s_cz, r_cz, s_cp, r_cp,
    s_da, r_da, s_db, r_db, s_pz, r_pz, s_pc, r_pc, s_dz, r_dz,
    s_co, r_co, s_x, r_x, s_z, r_z,
):
    d = lax.axis_index("dp")
    f = lax.axis_index("fsdp")
    xl = div(d, 2 * NZ)
    z = rem(div(d, 2), NZ)
    c = rem(d, 2)
    q = xl * 2 + c
    p = q * NF + f

    def dev(xx, zz, cc, ff):
        return ((xx * NZ + zz) * 2 + cc, ff)

    def plane(k):
        qq = rem(q + div(k, NF), 4)
        ff = rem(f + rem(k, NF), NF)
        return qq, ff, qq * NF + ff

    def copy(src, dst, ss, rs, to):
        return pltpu.make_async_remote_copy(
            src_ref=src, dst_ref=dst, send_sem=ss, recv_sem=rs, device_id=to, device_id_type=MESH
        )

    def each(lo, hi, fn):
        def step(k, carry):
            fn(k)
            return carry

        lax.fori_loop(lo, hi, step, 0)

    def load(n, src, dst):
        return pltpu.make_async_copy(src, dst, s_in.at[n])

    def load_tok(i):
        rows = pl.ds(pl.multiple_of(i * 256, 256), 256)
        return load(i, tok_h.at[rows], tok.at[rows])

    loads = [
        load(4 + n, src, dst)
        for n, (src, dst) in enumerate(
            [
                (tea_h, tea), (ng_h, ng), (win_h, win), (b_in_h, b_in),
                (wout_h, wout), (b_out_h, b_out), (fg_h, fg),
            ]
        )
    ]
    loads[0].start()
    loads[1].start()
    load_tok(0).start()
    loads[2].start()
    loads[3].start()
    each(1, 4, lambda i: load_tok(i).start())
    for item in loads[4:]:
        item.start()

    barrier = pltpu.get_barrier_semaphore()

    def sig_plane(k):
        qq, ff, _ = plane(k)
        pl.semaphore_signal(
            barrier, inc=1, device_id=dev(div(qq, 2), z, rem(qq, 2), ff), device_id_type=MESH
        )

    def sig_z(k):
        pl.semaphore_signal(
            barrier, inc=1, device_id=dev(xl, rem(z + k, NZ), c, f), device_id_type=MESH
        )

    each(1, NP, sig_plane)
    each(1, NZ, sig_z)

    loads[0].wait()
    teacher = tea[...].astype(F32)
    t_norm = jnp.sqrt(jnp.sum(teacher * teacher, axis=-1, keepdims=True) + 1e-06)
    target = teacher / t_norm
    for a in range(16):
        for b in range(3):
            lo = 384 * a + 128 * b
            tflat[b, pl.ds(a, 8, stride=16), :] = target[:, lo : lo + 128]
    tp[q] = jnp.concatenate([tflat[b] for b in range(3)], axis=1).astype(BF16)
    own_rows = pl.ds(pl.multiple_of(f * 16, 16), 16)
    own_target = jnp.concatenate([tflat[b, own_rows, :] for b in range(3)], axis=1).astype(BF16)
    trow[...] = own_target
    tj[z] = own_target

    for item in loads[1:4]:
        item.wait()
    gain = ng[...]
    bias = b_in[...]

    def forward(i):
        load_tok(i).wait()
        rows = pl.ds(pl.multiple_of(i * 256, 256), 256)
        x = tok[rows, :].astype(F32)
        tmean[pl.ds(2 * i, 1), :] = jnp.sum(x[:128], axis=0, keepdims=True) * (1.0 / PER_IMAGE)
        tmean[pl.ds(2 * i + 1, 1), :] = jnp.sum(x[128:], axis=0, keepdims=True) * (1.0 / PER_IMAGE)
        centered = x - jnp.mean(x, axis=-1, keepdims=True)
        inv = lax.rsqrt(jnp.mean(centered * centered, axis=-1, keepdims=True) + 1e-05)
        nb = (centered * inv * gain).astype(BF16)
        normed[rows, :] = nb
        act = dot(nb, win[...]) + bias
        pre[rows, :] = act
        g = 0.5 * act * (1.0 + gelu_parts(act))
        pooled_f[pl.ds(2 * i, 1), :] = jnp.sum(g[:128], axis=0, keepdims=True) * (1.0 / PER_IMAGE)
        pooled_f[pl.ds(2 * i + 1, 1), :] = jnp.sum(g[128:], axis=0, keepdims=True) * (
            1.0 / PER_IMAGE
        )

    each(0, 2, forward)
    pl.semaphore_wait(barrier, NP - 1 + NZ - 1)
    def tq_copy(k):
        qq = rem(q + k, 4)
        return copy(
            tp.at[q], tp.at[q], s_tq, r_tq, dev(div(qq, 2), z, rem(qq, 2), f)
        )

    def tz_copy(k):
        return copy(trow, tj.at[z], s_tz, r_tz, dev(xl, rem(z + k, NZ), c, f))

    each(1, NZ, lambda k: tz_copy(k).start())
    each(1, 4, lambda k: tq_copy(k).start())
    each(2, 4, forward)
    for item in loads[4:]:
        item.wait()
    pooled_b = pooled_f[...].astype(BF16)
    partial = dot_last(pooled_b, wout[...])
    mean_tok = tmean[...]
    for a in range(8):
        part64[pl.ds(a, 8, stride=8), :] = partial[:, 128 * a : 128 * a + 128]
        tm64[pl.ds(a, 8, stride=8), :] = mean_tok[:, 128 * a : 128 * a + 128]

    def c1_copy(k):
        ff = rem(f + k, NF)
        return copy(
            part64.at[pl.ds(pl.multiple_of(ff * 8, 8), 8)],
            c1b.at[f], s_c1, r_c1, (d, ff),
        )

    each(1, NF, lambda k: c1_copy(k).start())
    c1b[f] = part64[pl.ds(pl.multiple_of(f * 8, 8), 8), :]
    px[...] = pooled_b.astype(F32)

    def px_copy():
        return copy(px, pin, s_px, r_px, dev(1 - xl, z, c, f))

    px_copy().start()

    def slopes(i):
        rows = pl.ds(pl.multiple_of(i * 128, 128), 128)
        v = pre[rows, :]
        t = gelu_parts(v)
        slope[rows, :] = 0.5 * (1.0 + t) + 0.5 * v * (1.0 - t * t) * 0.7978845608 * (
            1.0 + 3.0 * 0.044715 * v * v
        )

    each(0, 8, slopes)

    def wait_from(dst, ss, rs):
        copy(dst, dst, ss, rs, (d, f)).wait_recv()

    def sent(src, ss, rs):
        copy(src, src, ss, rs, (d, f)).wait_send()

    wait_from(c1b.at[0 : NF - 1], s_c1, r_c1)
    embedding = jnp.sum(c1b[...], axis=0) + tm64[pl.ds(pl.multiple_of(f * 8, 8), 8), :] + b_out[...]
    final_gain = fg[...]

    def total(v):
        return jnp.sum(jnp.sum(v, axis=1, keepdims=True), axis=0, keepdims=True)

    cent = embedding - total(embedding) * (1.0 / D)
    inv_std = lax.rsqrt(total(cent * cent) * (1.0 / D) + 1e-05)
    n_emb = cent * inv_std
    unit = n_emb * final_gain
    unit_norm = jnp.sqrt(total(unit * unit) + 1e-06)
    unit_dir = unit / unit_norm
    student = unit_dir.astype(BF16).astype(F32)
    st_row[...] = student

    def cz_copy(k):
        return copy(st_row, sj.at[z], s_cz, r_cz, dev(xl, rem(z + k, NZ), c, f))

    def cp_copy(k):
        qq, ff, _ = plane(k)
        return copy(st_row, sp.at[p], s_cp, r_cp, dev(div(qq, 2), z, rem(qq, 2), ff))

    each(1, NZ, lambda k: cz_copy(k).start())
    each(1, NP, lambda k: cp_copy(k).start())
    sj[z] = student
    sp[p] = student

    wait_from(tp.at[0:3], s_tq, r_tq)
    wait_from(tj.at[0 : NZ - 1], s_tz, r_tz)
    tx = dot_last(tp[...].reshape(NP * 16, 384), tj[...].reshape(NZ * 16, 384))
    same = (iota(tx.shape, 0) % 16) == (iota(tx.shape, 1) % 16)
    tx = jnp.sum(jnp.where(same, tx, 0.0).reshape(NP, 16, NZ * 16), axis=1)
    spread = ((iota((NZ * 16, 128), 0) // 16) == (iota((NZ * 16, 128), 1) // 8)).astype(BF16)
    gram_t = dot_exact(tx, spread)

    def pz_copy(k):
        return copy(
            pout16, pall.at[c, z], s_pz, r_pz, dev(xl, rem(z + k, NZ), c, f)
        )

    wait_from(pin, s_px, r_px)
    mine, other = px[...], pin[...]
    first = xl == 0
    block16 = jnp.concatenate(
        [jnp.where(first, mine, other), jnp.where(first, other, mine)], axis=0
    ).astype(BF16)
    pout16[...] = block16
    pall[c, z] = block16

    wait_from(sp.at[0 : NP - 1], s_cp, r_cp)
    wait_from(sj.at[0 : NZ - 1], s_cz, r_cz)
    s_plane = sp[...].reshape(NP * 8, 128).astype(BF16)
    s_other = sj[...].reshape(NZ * 8, 128).astype(BF16)
    sx = dot_last(s_plane, s_other)
    diag = (iota(sx.shape, 0) % 8) == (iota(sx.shape, 1) % 8)
    sx = jnp.sum(jnp.where(diag, sx, 0.0).reshape(NP, 8, 128), axis=1)
    group = ((iota((128, 128), 0) // 8) == (iota((128, 128), 1) // 8)).astype(BF16)
    resid = dot_exact(sx, group) - gram_t
    share = total(resid * resid) * 0.125
    wide = jnp.broadcast_to(resid[:, None, :], (NP, 8, 128)).reshape(NP * 8, 128)
    wide = jnp.where(diag, wide, 0.0).astype(BF16)
    dref[...] = dot(wide, s_other).reshape(NP, 8, 128)

    def da_copy(k):
        qq, ff, pp = plane(k)
        return copy(dref.at[pp], da.at[p], s_da, r_da, dev(div(qq, 2), z, rem(qq, 2), ff))

    each(1, NP, lambda k: da_copy(k).start())
    da[p] = dref[p]
    each(1, NZ, lambda k: pz_copy(k).start())

    wait_from(da.at[0 : NP - 1], s_da, r_da)
    dstudent = (LOSS_SCALE * 4.0 / IMAGES) * jnp.sum(da[...], axis=0)
    dunit = (dstudent - unit_dir * total(unit_dir * dstudent)) / unit_norm
    gain_grad = dunit * final_gain
    dembed = inv_std * (
        gain_grad - total(gain_grad) * (1.0 / D) - n_emb * (total(gain_grad * n_emb) * (1.0 / D))
    )
    message = jnp.concatenate(
        [dembed.astype(BF16).astype(F32), jnp.broadcast_to(share, (8, 128))], axis=0
    )
    dmsg[...] = message

    def rows16(pp):
        return pl.ds(pl.multiple_of(pp * 16, 16), 16)

    def db_copy(k, near):
        qq, ff, _ = plane(k)
        return copy(
            dmsg, db.at[rows16(p)], s_db.at[near], r_db.at[near], dev(div(qq, 2), z, rem(qq, 2), ff)
        )

    each(1, NF, lambda k: db_copy(k, 0).start())
    each(NF, NP, lambda k: db_copy(k, 1).start())
    db[rows16(p), :] = message

    wait_from(db.at[0 : (NF - 1) * 16], s_db.at[0], r_db.at[0])
    block = jnp.concatenate(
        [db[pl.ds(q * (NF * 16) + a, 8, stride=16), :] for a in range(8)], axis=1
    ).astype(BF16)
    tmean[:, :HID] = dot(block, wout[...]) * (1.0 / PER_IMAGE)

    def hidden(i):
        rows = pl.ds(pl.multiple_of(i * PER_IMAGE, PER_IMAGE), PER_IMAGE)
        dhid[rows, :] = (tmean[pl.ds(i, 1), :HID] * slope[rows, :]).astype(BF16)

    each(0, 8, hidden)

    low = c == 0
    s_bit = rem(z, 2)
    w = div(z, 2)

    def co_copy(j):
        return copy(sib.at[j], coreb.at[j], s_co, r_co.at[j], dev(xl, z, 1 - c, f))

    def near_copy(t, h):
        xx = xl if t == 2 else 1 - xl
        zz = 2 * w + (s_bit if t == 1 else 1 - s_bit)
        return copy(
            xs.at[t, h], xb.at[h, t], s_x, r_x.at[h], dev(xx, zz, c, f)
        )

    def core_sum(j, bit):
        return own[j, bit] + coreb[j, bit].astype(F32)

    def near_send(j):
        wait_from(coreb.at[j], s_co, r_co.at[j])
        h = j % 2
        for t in (0, 1) if j < 2 else (2,):
            xs[t, h] = core_sum(j, s_bit if t == 1 else 1 - s_bit).astype(BF16)
            near_copy(t, h).start()

    for j in range(4):
        side = (1 - xl) if j < 2 else xl
        cols = pl.ds(pl.multiple_of(side * 512 + (j % 2) * 256, 256), 256)
        term = dot_first(normed[:, cols], dhid[...]).reshape(4, 2, 2, 16, HID)
        for bit in range(2):
            mine_t, other_t = term[:, bit, 0], term[:, bit, 1]
            own[j, bit] = jnp.where(low, mine_t, other_t)
            sib[j, bit] = jnp.where(low, other_t, mine_t).astype(BF16)
        co_copy(j).start()
        if j >= 1:
            near_send(j - 1)

    wait_from(db.at[0 : (NP - NF) * 16], s_db.at[1], r_db.at[1])
    loss_plane = jnp.zeros((8, 128), F32)
    for pp in range(NP):
        loss_plane = loss_plane + db[pp * 16 + 8 : pp * 16 + 16, :]
    flat = jnp.concatenate(
        [db[pl.ds(xl * 4 + a, NP, stride=16), :] for a in range(4)], axis=1
    ).astype(BF16)
    image = iota((NP, 128), 0)
    odd = rem(z, 2)
    lane = odd * 32 + ((image // 8) % 2) * 16 + (image // 16) * 8 + image % 8
    place = (lane == iota((NP, 128), 1)).astype(BF16)
    turned = dot_first(flat, place).reshape(NZ, 2, 16, 128)
    turned = jnp.where(low, turned[:, 0], turned[:, 1])
    part = loss_plane[0:1, :]
    high = part.astype(BF16).astype(F32)
    mid = (part - high).astype(BF16).astype(F32)
    last = part - high - mid
    at = iota((1, 128), 1) - (64 + 4 * odd)
    extra = jnp.where(at == 0, high, jnp.where(at == 1, mid, jnp.where(at == 2, last, 0.0)))
    zmsg[...] = (turned + extra[None]).astype(BF16)
    dz[z] = zmsg[z]

    def dz_copy(k):
        zz = rem(z + k, NZ)
        return copy(zmsg.at[zz], dz.at[z], s_dz, r_dz, dev(xl, zz, c, f))

    each(1, NZ, lambda k: dz_copy(k).start())

    near_send(3)

    def z_copy(k):
        ww = rem(w + k, NW)
        return copy(zs.at[ww], zb.at[w], s_z, r_z, dev(xl, 2 * ww + s_bit, c, f))

    def z_start(k):
        z_copy(k).start()

    zb[w] = jnp.zeros((16, HID), BF16)
    for h in range(2):
        merged = core_sum(2 + h, s_bit)
        wait_from(xb.at[h], s_x, r_x.at[h])
        for t in range(3):
            merged = merged + xb[h, t].astype(F32)
        totf[4 * h : 4 * h + 4] = merged
        zs[4 * h : 4 * h + 4] = merged.astype(BF16)
        for ww in range(4 * h, 4 * h + 4):
            k = rem(ww + NW - w, NW)

            @pl.when(k != 0)
            def _():
                z_start(k)

    wait_from(pall.at[c, 0 : NZ - 1], s_pz, r_pz)

    def pc_copy():
        return copy(pall.at[c], pall.at[c], s_pc, r_pc, dev(xl, z, 1 - c, f))

    pc_copy().start()

    wait_from(dz.at[0 : NZ - 1], s_dz, r_dz)
    wait_from(pall.at[1 - c], s_pc, r_pc)
    acc = jnp.zeros((16, HID), F32)
    loss = jnp.zeros((16, 128), F32)
    for g in range(NZ // 2):
        left = dz[2 * g].astype(F32) + dz[2 * g + 1].astype(F32)
        loss = loss + left
        right = jnp.concatenate(
            [pall[cc, zz] for zz in (2 * g, 2 * g + 1) for cc in range(2)], axis=0
        )
        acc = acc + dot(left[:, :64].astype(BF16), right)
    out_ref[16:32, :] = acc.astype(BF16)
    loss = jnp.sum(jnp.where(iota((16, 128), 1) >= 64, loss, 0.0), axis=1, keepdims=True)
    loss_ref[...] = loss[:1, :] * (1.0 / IMAGES)

    sent(tp.at[0:3], s_tq, r_tq)
    sent(tj.at[0 : NZ - 1], s_tz, r_tz)
    sent(c1b.at[0 : NF - 1], s_c1, r_c1)
    sent(px, s_px, r_px)
    sent(sj.at[0 : NZ - 1], s_cz, r_cz)
    sent(sp.at[0 : NP - 1], s_cp, r_cp)
    sent(da.at[0 : NP - 1], s_da, r_da)
    sent(pall.at[c, 0 : NZ - 1], s_pz, r_pz)
    sent(db.at[0 : (NF - 1) * 16], s_db.at[0], r_db.at[0])
    sent(db.at[0 : (NP - NF) * 16], s_db.at[1], r_db.at[1])
    sent(dz.at[0 : NZ - 1], s_dz, r_dz)
    sent(sib, s_co, r_co.at[0])
    sent(xs, s_x, r_x.at[0])
    sent(pall.at[c], s_pc, r_pc)

    wait_from(zb.at[0 : NW - 1], s_z, r_z)
    out_ref[0:16, :] = (totf[w] + jnp.sum(zb[...].astype(F32), axis=0)).astype(BF16)
    sent(zb.at[0 : NW - 1], s_z, r_z)


def body(tokens, teacher, norm_gain, w_in, b_in, w_out, b_out, final_gain):
    vmem = pl.BlockSpec(memory_space=pltpu.VMEM)
    one, two, four = (
        pltpu.SemaphoreType.DMA, pltpu.SemaphoreType.DMA((2,)), pltpu.SemaphoreType.DMA((4,))
    )
    sems = [one, one] * 7 + [two, two] + [one, one] * 3 + [one, four] + [one, two] + [one, one]
    packed, loss = pl.pallas_call(
        kernel,
        name="gram_step",
        out_shape=(
            jax.ShapeDtypeStruct((32, HID), BF16),
            jax.ShapeDtypeStruct((1, 1), F32),
        ),
        in_specs=[pl.BlockSpec(memory_space=pl.ANY)] * 8,
        out_specs=(vmem, vmem),
        scratch_shapes=[
            pltpu.VMEM((1024, D), BF16),
            pltpu.VMEM((8, DT), BF16),
            pltpu.VMEM((1, D), F32),
            pltpu.VMEM((D, HID), BF16),
            pltpu.VMEM((1, HID), F32),
            pltpu.VMEM((D, HID), BF16),
            pltpu.VMEM((8, 128), F32),
            pltpu.VMEM((8, 128), F32),
            pltpu.SemaphoreType.DMA((11,)),
            pltpu.VMEM((1024, D), BF16),
            pltpu.VMEM((1024, HID), F32),
            pltpu.VMEM((1024, HID), F32),
            pltpu.VMEM((1024, HID), BF16),
            pltpu.VMEM((8, D), F32),
            pltpu.VMEM((8, HID), F32),
            pltpu.VMEM((64, 128), F32),
            pltpu.VMEM((64, 128), F32),
            pltpu.VMEM((3, 128, 128), F32),
            pltpu.VMEM((4, 128, 384), BF16),
            pltpu.VMEM((NZ, 16, 384), BF16),
            pltpu.VMEM((16, 384), BF16),
            pltpu.VMEM((NF, 8, 128), F32),
            pltpu.VMEM((8, 128), F32),
            pltpu.VMEM((NP, 8, 128), F32),
            pltpu.VMEM((NZ, 8, 128), F32),
            pltpu.VMEM((NP, 8, 128), F32),
            pltpu.VMEM((NP, 8, 128), F32),
            pltpu.VMEM((16, 128), F32),
            pltpu.VMEM((NP * 16, 128), F32),
            pltpu.VMEM((8, HID), F32),
            pltpu.VMEM((8, HID), F32),
            pltpu.VMEM((16, HID), BF16),
            pltpu.VMEM((2, NZ, 16, HID), BF16),
            pltpu.VMEM((NZ, 16, 128), BF16),
            pltpu.VMEM((NZ, 16, 128), BF16),
            pltpu.VMEM((4, 2, 4, 16, HID), F32),
            pltpu.VMEM((4, 2, 4, 16, HID), BF16),
            pltpu.VMEM((4, 2, 4, 16, HID), BF16),
            pltpu.VMEM((3, 2, 4, 16, HID), BF16),
            pltpu.VMEM((2, 3, 4, 16, HID), BF16),
            pltpu.VMEM((NW, 16, HID), F32),
            pltpu.VMEM((NW, 16, HID), BF16),
            pltpu.VMEM((NW, 16, HID), BF16),
        ]
        + sems,
        compiler_params=pltpu.CompilerParams(
            collective_id=0, has_side_effects=True, vmem_limit_bytes=56 << 20
        ),
        cost_estimate=pl.CostEstimate(
            flops=5_000_000_000, bytes_accessed=8_000_000, transcendentals=1_000_000
        ),
    )(
        tokens,
        teacher,
        norm_gain.reshape(1, D),
        w_in,
        b_in.reshape(1, HID),
        w_out,
        b_out.reshape(8, 128),
        final_gain.reshape(8, 128),
    )
    return loss.reshape(()), packed[:16], packed[16:]


def solution(mesh):
    return jax.shard_map(
        body,
        mesh=mesh,
        in_specs=(
            P("dp", None),
            P("dp", None),
            P(),
            P(None, "fsdp"),
            P("fsdp"),
            P(None, "fsdp"),
            P(),
            P(),
        ),
        out_specs=(P(), P("dp", "fsdp"), P("dp", "fsdp")),
        check_vma=False,
    )
```

```python
import jax
import jax.numpy as jnp
from jax import lax
from jax.experimental import pallas as pl
from jax.experimental.pallas import tpu as pltpu
from jax.sharding import PartitionSpec as P

MESH = pl.DeviceIdType.MESH
F32 = jnp.float32
BF16 = jnp.bfloat16

NZ = 16
NF = 8
NW = 8
NP = 32
LOSS_SCALE = 4096.0
IMAGES = 512
PER_IMAGE = 128
D = 1024
DT = 6144
HID = 512


def dot(left, right):
    return jnp.dot(left, right, preferred_element_type=F32)


def dot_last(left, right):
    return lax.dot_general(left, right, (((1,), (1,)), ((), ())), preferred_element_type=F32)


def dot_first(left, right):
    return lax.dot_general(left, right, (((0,), (0,)), ((), ())), preferred_element_type=F32)


def dot_exact(values, ones):
    high = values.astype(BF16)
    rest = values - high.astype(F32)
    mid = rest.astype(BF16)
    low = (rest - mid.astype(F32)).astype(BF16)
    return dot(high, ones) + dot(mid, ones) + dot(low, ones)


def div(value, by):
    return lax.div(value, jnp.int32(by))


def rem(value, by):
    return lax.rem(value, jnp.int32(by))


def iota(shape, axis):
    return lax.broadcasted_iota(jnp.int32, shape, axis)


def gelu_parts(values):
    inner = 0.7978845608 * (values + 0.044715 * values * values * values)
    return jnp.tanh(inner)


def kernel(
    tok_h, tea_h, ng_h, win_h, b_in_h, wout_h, b_out_h, fg_h,
    loss_ref, gin_ref, gout_ref,
    tok, tea, ng, win, b_in, wout, b_out, fg, s_in,
    normed, normed_t, pre, slope, dhid, tmean, pooled_f, part64, tm64,
    tflat, tp, tj, trow, c1b, st_row, sp, sj, dref, da, dmsg, db,
    px, pin, pout16, pall, zmsg, dz,
    own, sib, coreb, xs, xb, xm, xn, totf, zs, zb,
    s_tq, r_tq, s_tz, r_tz, s_c1, r_c1, s_px, r_px, s_cz, r_cz, s_cp, r_cp,
    s_da, r_da, s_db, r_db, s_pz, r_pz, s_pc, r_pc, s_dz, r_dz,
    s_co, r_co, s_x, r_x, s_xm, r_xm, s_z, r_z,
):
    d = lax.axis_index("dp")
    f = lax.axis_index("fsdp")
    xl = div(d, 2 * NZ)
    z = rem(div(d, 2), NZ)
    c = rem(d, 2)
    q = xl * 2 + c
    p = q * NF + f

    def dev(xx, zz, cc, ff):
        return ((xx * NZ + zz) * 2 + cc, ff)

    def plane(k):
        qq = rem(q + div(k, NF), 4)
        ff = rem(f + rem(k, NF), NF)
        return qq, ff, qq * NF + ff

    def copy(src, dst, ss, rs, to):
        return pltpu.make_async_remote_copy(
            src_ref=src, dst_ref=dst, send_sem=ss, recv_sem=rs, device_id=to, device_id_type=MESH
        )

    def each(lo, hi, fn):
        def step(k, carry):
            fn(k)
            return carry

        lax.fori_loop(lo, hi, step, 0)

    def along_z(fn):
        def step(m, carry):
            fn(NZ // 2 + div(m + 1, 2) * (1 - 2 * rem(m, 2)))
            return carry

        lax.fori_loop(0, NZ - 1, step, 0)

    def load(n, src, dst):
        return pltpu.make_async_copy(src, dst, s_in.at[n])

    def load_tok(i):
        rows = pl.ds(pl.multiple_of(i * 256, 256), 256)
        return load(i, tok_h.at[rows], tok.at[rows])

    loads = [
        load(4 + n, src, dst)
        for n, (src, dst) in enumerate(
            [
                (tea_h, tea), (ng_h, ng), (win_h, win), (b_in_h, b_in),
                (wout_h, wout), (b_out_h, b_out), (fg_h, fg),
            ]
        )
    ]
    loads[0].start()
    loads[1].start()
    load_tok(0).start()
    loads[2].start()
    loads[3].start()
    each(1, 4, lambda i: load_tok(i).start())
    for item in loads[4:]:
        item.start()

    barrier = pltpu.get_barrier_semaphore()

    def sig_plane(k):
        qq, ff, _ = plane(k)
        pl.semaphore_signal(
            barrier, inc=1, device_id=dev(div(qq, 2), z, rem(qq, 2), ff), device_id_type=MESH
        )

    def sig_z(k):
        pl.semaphore_signal(
            barrier, inc=1, device_id=dev(xl, rem(z + k, NZ), c, f), device_id_type=MESH
        )

    for m in range(NZ - 1):
        sig_z(NZ // 2 + (m + 1) // 2 * (1 - 2 * (m % 2)))
    for k in range(1, NP):
        sig_plane(k)

    loads[0].wait()
    teacher = tea[...].astype(F32)
    t_norm = jnp.sqrt(jnp.sum(teacher * teacher, axis=-1, keepdims=True) + 1e-06)
    target = teacher / t_norm
    for a in range(16):
        for b in range(3):
            lo = 384 * a + 128 * b
            tflat[b, pl.ds(a, 8, stride=16), :] = target[:, lo : lo + 128]
    tp[q] = jnp.concatenate([tflat[b] for b in range(3)], axis=1).astype(BF16)
    own_rows = pl.ds(pl.multiple_of(f * 16, 16), 16)
    own_target = jnp.concatenate([tflat[b, own_rows, :] for b in range(3)], axis=1).astype(BF16)
    trow[...] = own_target
    tj[z] = own_target

    for item in loads[1:4]:
        item.wait()
    gain = ng[...]
    bias = b_in[...]

    def normalise(i):
        rows = slice(256 * i, 256 * i + 256)
        x = tok[rows, :].astype(F32)
        for n in range(2):
            tmean[2 * i + n : 2 * i + n + 1, :] = jnp.sum(
                x[128 * n : 128 * n + 128], axis=0, keepdims=True
            ) * (1.0 / PER_IMAGE)
        centered = x - jnp.mean(x, axis=-1, keepdims=True)
        inv = lax.rsqrt(jnp.mean(centered * centered, axis=-1, keepdims=True) + 1e-05)
        normed[rows, :] = (centered * inv * gain).astype(BF16)

    def activate(i):
        rows = slice(256 * i, 256 * i + 256)
        act = dot(normed[rows, :], win[...]) + bias
        pre[rows, :] = act
        g = 0.5 * act * (1.0 + gelu_parts(act))
        for n in range(2):
            pooled_f[2 * i + n : 2 * i + n + 1, :] = jnp.sum(
                g[128 * n : 128 * n + 128], axis=0, keepdims=True
            ) * (1.0 / PER_IMAGE)

    load_tok(0).wait()
    normalise(0)
    load_tok(1).wait()
    activate(0)
    normalise(1)
    pl.semaphore_wait(barrier, NP - 1 + NZ - 1)
    def tq_copy(k):
        qq = rem(q + k, 4)
        return copy(
            tp.at[q], tp.at[q], s_tq, r_tq, dev(div(qq, 2), z, rem(qq, 2), f)
        )

    def tz_copy(k):
        return copy(trow, tj.at[z], s_tz, r_tz, dev(xl, rem(z + k, NZ), c, f))

    along_z(lambda k: tz_copy(k).start())
    load_tok(2).wait()
    activate(1)
    normalise(2)
    load_tok(3).wait()
    activate(2)
    normalise(3)
    activate(3)
    for item in loads[4:]:
        item.wait()
    pooled_b = pooled_f[...].astype(BF16)
    partial = dot_last(pooled_b, wout[...])
    mean_tok = tmean[...]
    for a in range(8):
        part64[pl.ds(a, 8, stride=8), :] = partial[:, 128 * a : 128 * a + 128]
        tm64[pl.ds(a, 8, stride=8), :] = mean_tok[:, 128 * a : 128 * a + 128]

    def c1_copy(k):
        ff = rem(f + k, NF)
        return copy(
            part64.at[pl.ds(pl.multiple_of(ff * 8, 8), 8)],
            c1b.at[f], s_c1, r_c1, (d, ff),
        )

    each(1, NF, lambda k: c1_copy(k).start())
    c1b[f] = part64[pl.ds(pl.multiple_of(f * 8, 8), 8), :]
    px[...] = pooled_b.astype(F32)

    def px_copy():
        return copy(px, pin, s_px, r_px, dev(1 - xl, z, c, f))

    px_copy().start()
    each(1, 4, lambda k: tq_copy(k).start())

    def slopes(i):
        rows = pl.ds(pl.multiple_of(i * 128, 128), 128)
        v = pre[rows, :]
        t = gelu_parts(v)
        slope[rows, :] = 0.5 * (1.0 + t) + 0.5 * v * (1.0 - t * t) * 0.7978845608 * (
            1.0 + 3.0 * 0.044715 * v * v
        )

    each(0, 8, slopes)

    def wait_from(dst, ss, rs):
        copy(dst, dst, ss, rs, (d, f)).wait_recv()

    def sent(src, ss, rs):
        copy(src, src, ss, rs, (d, f)).wait_send()

    wait_from(c1b.at[0 : NF - 1], s_c1, r_c1)
    embedding = jnp.sum(c1b[...], axis=0) + tm64[pl.ds(pl.multiple_of(f * 8, 8), 8), :] + b_out[...]
    final_gain = fg[...]

    def total(v):
        return jnp.sum(jnp.sum(v, axis=1, keepdims=True), axis=0, keepdims=True)

    cent = embedding - total(embedding) * (1.0 / D)
    inv_std = lax.rsqrt(total(cent * cent) * (1.0 / D) + 1e-05)
    n_emb = cent * inv_std
    unit = n_emb * final_gain
    unit_norm = jnp.sqrt(total(unit * unit) + 1e-06)
    unit_dir = unit / unit_norm
    student = unit_dir.astype(BF16).astype(F32)
    st_row[...] = student

    def cz_copy(k):
        return copy(st_row, sj.at[z], s_cz, r_cz, dev(xl, rem(z + k, NZ), c, f))

    def cp_copy(k):
        qq, ff, _ = plane(k)
        return copy(st_row, sp.at[p], s_cp, r_cp, dev(div(qq, 2), z, rem(qq, 2), ff))

    along_z(lambda k: cz_copy(k).start())
    each(1, NP, lambda k: cp_copy(k).start())
    sj[z] = student
    sp[p] = student

    wait_from(tp.at[0:3], s_tq, r_tq)
    wait_from(tj.at[0 : NZ - 1], s_tz, r_tz)
    tx = dot_last(tp[...].reshape(NP * 16, 384), tj[...].reshape(NZ * 16, 384))
    same = (iota(tx.shape, 0) % 16) == (iota(tx.shape, 1) % 16)
    tx = jnp.sum(jnp.where(same, tx, 0.0).reshape(NP, 16, NZ * 16), axis=1)
    spread = ((iota((NZ * 16, 128), 0) // 16) == (iota((NZ * 16, 128), 1) // 8)).astype(BF16)
    gram_t = dot_exact(tx, spread)

    def pz_copy(k):
        return copy(
            pout16, pall.at[c, z], s_pz, r_pz, dev(xl, rem(z + k, NZ), c, f)
        )

    wait_from(pin, s_px, r_px)
    mine, other = px[...], pin[...]
    first = xl == 0
    block16 = jnp.concatenate(
        [jnp.where(first, mine, other), jnp.where(first, other, mine)], axis=0
    ).astype(BF16)
    pout16[...] = block16
    pall[c, z] = block16

    for i in range(4):
        turned_cols = slice(256 * i, 256 * i + 256)
        normed_t[turned_cols, :] = normed[:, turned_cols].T

    wait_from(sp.at[0 : NP - 1], s_cp, r_cp)
    wait_from(sj.at[0 : NZ - 1], s_cz, r_cz)
    s_plane = sp[...].reshape(NP * 8, 128).astype(BF16)
    s_other = sj[...].reshape(NZ * 8, 128).astype(BF16)
    sx = dot_last(s_plane, s_other)
    diag = (iota(sx.shape, 0) % 8) == (iota(sx.shape, 1) % 8)
    sx = jnp.sum(jnp.where(diag, sx, 0.0).reshape(NP, 8, 128), axis=1)
    group = ((iota((128, 128), 0) // 8) == (iota((128, 128), 1) // 8)).astype(BF16)
    resid = dot_exact(sx, group) - gram_t
    share = total(resid * resid) * 0.125
    wide = jnp.broadcast_to(resid[:, None, :], (NP, 8, 128)).reshape(NP * 8, 128)
    wide = jnp.where(diag, wide, 0.0).astype(BF16)
    dref[...] = dot(wide, s_other).reshape(NP, 8, 128)

    def da_copy(k):
        qq, ff, pp = plane(k)
        return copy(dref.at[pp], da.at[p], s_da, r_da, dev(div(qq, 2), z, rem(qq, 2), ff))

    each(1, NP, lambda k: da_copy(k).start())
    da[p] = dref[p]
    along_z(lambda k: pz_copy(k).start())

    wait_from(da.at[0 : NP - 1], s_da, r_da)
    dstudent = (LOSS_SCALE * 4.0 / IMAGES) * jnp.sum(da[...], axis=0)
    dunit = (dstudent - unit_dir * total(unit_dir * dstudent)) / unit_norm
    gain_grad = dunit * final_gain
    dembed = inv_std * (
        gain_grad - total(gain_grad) * (1.0 / D) - n_emb * (total(gain_grad * n_emb) * (1.0 / D))
    )
    message = jnp.concatenate(
        [dembed.astype(BF16).astype(F32), jnp.broadcast_to(share, (8, 128))], axis=0
    )
    dmsg[...] = message

    def rows16(pp):
        return pl.ds(pl.multiple_of(pp * 16, 16), 16)

    def db_copy(k, near):
        qq, ff, _ = plane(k)
        return copy(
            dmsg, db.at[rows16(p)], s_db.at[near], r_db.at[near], dev(div(qq, 2), z, rem(qq, 2), ff)
        )

    each(1, NF, lambda k: db_copy(k, 0).start())
    each(NF, NP, lambda k: db_copy(k, 1).start())
    db[rows16(p), :] = message

    wait_from(db.at[0 : (NF - 1) * 16], s_db.at[0], r_db.at[0])
    block = jnp.concatenate(
        [db[pl.ds(q * (NF * 16) + a, 8, stride=16), :] for a in range(8)], axis=1
    ).astype(BF16)
    tmean[:, :HID] = dot(block, wout[...]) * (1.0 / PER_IMAGE)

    def hidden(i):
        rows = pl.ds(pl.multiple_of(i * PER_IMAGE, PER_IMAGE), PER_IMAGE)
        dhid[rows, :] = (tmean[pl.ds(i, 1), :HID] * slope[rows, :]).astype(BF16)

    each(0, 8, hidden)

    low = c == 0
    s_bit = rem(z, 2)
    w = div(z, 2)

    def half(h):
        return rem(div(w, 4) + 1 + h, 2)

    def co_copy(j):
        return copy(sib.at[j], coreb.at[j], s_co, r_co.at[j], dev(xl, z, 1 - c, f))

    step = 1 - 2 * s_bit

    def near_copy(t, h):
        xx = xl if t >= 3 else 1 - xl
        zz = z if t == 2 else rem(z + NZ + (step if t in (0, 3) else -step), NZ)
        if t == 2:
            return copy(xm.at[h], xn.at[h], s_xm, r_xm.at[h], dev(xx, zz, c, f))
        n = t if t < 2 else t - 1
        return copy(xs.at[n, h], xb.at[h, n], s_x, r_x.at[h], dev(xx, zz, c, f))

    def core_sum(j, bit):
        return own[j, bit] + coreb[j, bit].astype(F32)

    def near_send(j):
        wait_from(coreb.at[j], s_co, r_co.at[j])
        h = half(j % 2)
        across = core_sum(j, 1 - s_bit).astype(BF16)
        first = 0 if j < 2 else 2
        for n in range(2):
            xs[first + n, h] = across[:, :, 256 * n : 256 * n + 256]
        if j < 2:
            near_copy(0, h).start()
            near_copy(1, h).start()
            xm[h] = core_sum(j, s_bit).astype(BF16)
            near_copy(2, h).start()
        else:
            near_copy(3, h).start()
            near_copy(4, h).start()

    def dz_copy(k):
        zz = rem(z + k, NZ)
        return copy(zmsg.at[zz], dz.at[z], s_dz, r_dz, dev(xl, zz, c, f))

    def turn():
        wait_from(db.at[0 : (NP - NF) * 16], s_db.at[1], r_db.at[1])
        loss_plane = jnp.zeros((8, 128), F32)
        for pp in range(NP):
            loss_plane = loss_plane + db[pp * 16 + 8 : pp * 16 + 16, :]
        flat = jnp.concatenate(
            [db[pl.ds(xl * 4 + a, NP, stride=16), :] for a in range(4)], axis=1
        ).astype(BF16)
        image = iota((NP, 128), 0)
        odd = rem(z, 2)
        lane = odd * 32 + ((image // 8) % 2) * 16 + (image // 16) * 8 + image % 8
        place = (lane == iota((NP, 128), 1)).astype(BF16)
        turned = dot_first(flat, place).reshape(NZ, 2, 16, 128)
        turned = jnp.where(low, turned[:, 0], turned[:, 1])
        part = loss_plane[0:1, :]
        high = part.astype(BF16).astype(F32)
        mid = (part - high).astype(BF16).astype(F32)
        last = part - high - mid
        at = iota((1, 128), 1) - (64 + 4 * odd)
        extra = jnp.where(at == 0, high, jnp.where(at == 1, mid, jnp.where(at == 2, last, 0.0)))
        zmsg[...] = (turned + extra[None]).astype(BF16)
        dz[z] = zmsg[z]
        along_z(lambda k: dz_copy(k).start())

    for j in range(4):
        side = (1 - xl) if j < 2 else xl
        cols = pl.ds(pl.multiple_of(side * 512 + half(j % 2) * 256, 256), 256)
        term = dot(normed_t[cols, :], dhid[...]).reshape(4, 2, 2, 16, HID)
        for bit in range(2):
            mine_t, other_t = term[:, bit, 0], term[:, bit, 1]
            own[j, bit] = jnp.where(low, mine_t, other_t)
            sib[j, bit] = jnp.where(low, other_t, mine_t).astype(BF16)
        co_copy(j).start()
        if j >= 1:
            near_send(j - 1)
        if j == 2:
            turn()

    near_send(3)

    def z_copy(k):
        ww = rem(w + k, NW)
        return copy(zs.at[ww], zb.at[w], s_z, r_z, dev(xl, 2 * ww + s_bit, c, f))

    zb[w] = jnp.zeros((16, HID), BF16)
    for h in range(2):
        merged = core_sum(2 + h, s_bit)
        hh = half(h)
        wait_from(xn.at[hh], s_xm, r_xm.at[hh])
        merged = merged + xn[hh].astype(F32)
        wait_from(xb.at[hh], s_x, r_x.at[hh])
        sides = [xb[hh, n].astype(F32) + xb[hh, 2 + n].astype(F32) for n in range(2)]
        merged = merged + jnp.concatenate(sides, axis=2)
        blocks = pl.ds(hh * 4, 4)
        totf[blocks] = merged
        zs[blocks] = merged.astype(BF16)
        for k in (4, 3, 5, 2, 6, 1, 7):

            @pl.when(div(rem(w + k, NW), 4) == hh)
            def _():
                z_copy(k).start()

    wait_from(pall.at[c, 0 : NZ - 1], s_pz, r_pz)

    def pc_copy():
        return copy(pall.at[c], pall.at[c], s_pc, r_pc, dev(xl, z, 1 - c, f))

    pc_copy().start()

    wait_from(dz.at[0 : NZ - 1], s_dz, r_dz)
    wait_from(pall.at[1 - c], s_pc, r_pc)
    acc = jnp.zeros((16, HID), F32)
    loss = jnp.zeros((16, 128), F32)
    for g in range(NZ // 2):
        left = dz[2 * g].astype(F32) + dz[2 * g + 1].astype(F32)
        loss = loss + left
        right = jnp.concatenate(
            [pall[cc, zz] for zz in (2 * g, 2 * g + 1) for cc in range(2)], axis=0
        )
        acc = acc + dot(left[:, :64].astype(BF16), right)
    gout_ref[...] = acc.astype(BF16)
    loss = jnp.sum(jnp.where(iota((16, 128), 1) >= 64, loss, 0.0), axis=1, keepdims=True)
    loss_ref[...] = jnp.broadcast_to(loss[:8], (8, 128)) * (1.0 / IMAGES)

    sent(tp.at[0:3], s_tq, r_tq)
    sent(tj.at[0 : NZ - 1], s_tz, r_tz)
    sent(c1b.at[0 : NF - 1], s_c1, r_c1)
    sent(px, s_px, r_px)
    sent(sj.at[0 : NZ - 1], s_cz, r_cz)
    sent(sp.at[0 : NP - 1], s_cp, r_cp)
    sent(da.at[0 : NP - 1], s_da, r_da)
    sent(pall.at[c, 0 : NZ - 1], s_pz, r_pz)
    sent(db.at[0 : (NF - 1) * 16], s_db.at[0], r_db.at[0])
    sent(db.at[0 : (NP - NF) * 16], s_db.at[1], r_db.at[1])
    sent(dz.at[0 : NZ - 1], s_dz, r_dz)
    sent(sib, s_co, r_co.at[0])
    sent(xs, s_x, r_x.at[0])
    sent(xm, s_xm, r_xm.at[0])
    sent(pall.at[c], s_pc, r_pc)

    wait_from(zb.at[0 : NW - 1], s_z, r_z)
    gin_ref[...] = (totf[w] + jnp.sum(zb[...].astype(F32), axis=0)).astype(BF16)
    sent(zb.at[0 : NW - 1], s_z, r_z)


def body(tokens, teacher, norm_gain, w_in, b_in, w_out, b_out, final_gain):
    vmem = pl.BlockSpec(memory_space=pltpu.VMEM)
    one, two, four = (
        pltpu.SemaphoreType.DMA, pltpu.SemaphoreType.DMA((2,)), pltpu.SemaphoreType.DMA((4,))
    )
    sems = [one, one] * 7 + [two, two] + [one, one] * 3 + [one, four] + [one, two] * 2 + [one, one]
    loss, grad_in, grad_out = pl.pallas_call(
        kernel,
        name="gram_step",
        out_shape=(
            jax.ShapeDtypeStruct((8, 128), F32),
            jax.ShapeDtypeStruct((16, HID), BF16),
            jax.ShapeDtypeStruct((16, HID), BF16),
        ),
        in_specs=[pl.BlockSpec(memory_space=pl.ANY)] * 8,
        out_specs=(vmem, vmem, vmem),
        scratch_shapes=[
            pltpu.VMEM((1024, D), BF16),
            pltpu.VMEM((8, DT), BF16),
            pltpu.VMEM((1, D), F32),
            pltpu.VMEM((D, HID), BF16),
            pltpu.VMEM((1, HID), F32),
            pltpu.VMEM((D, HID), BF16),
            pltpu.VMEM((8, 128), F32),
            pltpu.VMEM((8, 128), F32),
            pltpu.SemaphoreType.DMA((11,)),
            pltpu.VMEM((1024, D), BF16),
            pltpu.VMEM((D, 1024), BF16),
            pltpu.VMEM((1024, HID), F32),
            pltpu.VMEM((1024, HID), F32),
            pltpu.VMEM((1024, HID), BF16),
            pltpu.VMEM((8, D), F32),
            pltpu.VMEM((8, HID), F32),
            pltpu.VMEM((64, 128), F32),
            pltpu.VMEM((64, 128), F32),
            pltpu.VMEM((3, 128, 128), F32),
            pltpu.VMEM((4, 128, 384), BF16),
            pltpu.VMEM((NZ, 16, 384), BF16),
            pltpu.VMEM((16, 384), BF16),
            pltpu.VMEM((NF, 8, 128), F32),
            pltpu.VMEM((8, 128), F32),
            pltpu.VMEM((NP, 8, 128), F32),
            pltpu.VMEM((NZ, 8, 128), F32),
            pltpu.VMEM((NP, 8, 128), F32),
            pltpu.VMEM((NP, 8, 128), F32),
            pltpu.VMEM((16, 128), F32),
            pltpu.VMEM((NP * 16, 128), F32),
            pltpu.VMEM((8, HID), F32),
            pltpu.VMEM((8, HID), F32),
            pltpu.VMEM((16, HID), BF16),
            pltpu.VMEM((2, NZ, 16, HID), BF16),
            pltpu.VMEM((NZ, 16, 128), BF16),
            pltpu.VMEM((NZ, 16, 128), BF16),
            pltpu.VMEM((4, 2, 4, 16, HID), F32),
            pltpu.VMEM((4, 2, 4, 16, HID), BF16),
            pltpu.VMEM((4, 2, 4, 16, HID), BF16),
            pltpu.VMEM((4, 2, 4, 16, HID // 2), BF16),
            pltpu.VMEM((2, 4, 4, 16, HID // 2), BF16),
            pltpu.VMEM((2, 4, 16, HID), BF16),
            pltpu.VMEM((2, 4, 16, HID), BF16),
            pltpu.VMEM((NW, 16, HID), F32),
            pltpu.VMEM((NW, 16, HID), BF16),
            pltpu.VMEM((NW, 16, HID), BF16),
        ]
        + sems,
        compiler_params=pltpu.CompilerParams(
            collective_id=0, has_side_effects=True, vmem_limit_bytes=56 << 20
        ),
        cost_estimate=pl.CostEstimate(
            flops=5_000_000_000, bytes_accessed=8_000_000, transcendentals=1_000_000
        ),
    )(
        tokens,
        teacher,
        norm_gain.reshape(1, D),
        w_in,
        b_in.reshape(1, HID),
        w_out,
        b_out.reshape(8, 128),
        final_gain.reshape(8, 128),
    )
    return loss[0, 0], grad_in, grad_out


def solution(mesh):
    return jax.shard_map(
        body,
        mesh=mesh,
        in_specs=(
            P("dp", None),
            P("dp", None),
            P(),
            P(None, "fsdp"),
            P("fsdp"),
            P(None, "fsdp"),
            P(),
            P(),
        ),
        out_specs=(P(), P("dp", "fsdp"), P("dp", "fsdp")),
        check_vma=False,
    )
```

```python
import jax
import jax.numpy as jnp
from jax import lax
from jax.experimental import pallas as pl
from jax.experimental.pallas import tpu as pltpu
from jax.sharding import PartitionSpec as P

MESH = pl.DeviceIdType.MESH
F32 = jnp.float32
BF16 = jnp.bfloat16

NZ = 16
NF = 8
NW = 8
NP = 32
LOSS_SCALE = 4096.0
IMAGES = 512
PER_IMAGE = 128
D = 1024
DT = 6144
HID = 512


def dot(left, right):
    return jnp.dot(left, right, preferred_element_type=F32)


def dot_last(left, right):
    return lax.dot_general(left, right, (((1,), (1,)), ((), ())), preferred_element_type=F32)


def dot_first(left, right):
    return lax.dot_general(left, right, (((0,), (0,)), ((), ())), preferred_element_type=F32)


def dot_exact(values, ones):
    high = values.astype(BF16)
    rest = values - high.astype(F32)
    mid = rest.astype(BF16)
    low = (rest - mid.astype(F32)).astype(BF16)
    return dot(high, ones) + dot(mid, ones) + dot(low, ones)


def div(value, by):
    return lax.div(value, jnp.int32(by))


def rem(value, by):
    return lax.rem(value, jnp.int32(by))


def iota(shape, axis):
    return lax.broadcasted_iota(jnp.int32, shape, axis)


def gelu_parts(values):
    inner = 0.7978845608 * (values + 0.044715 * values * values * values)
    return jnp.tanh(inner)


def kernel(
    tok_h, tea_h, ng_h, win_h, b_in_h, wout_h, b_out_h, fg_h,
    out_ref, loss_ref,
    tok, tea, ng, win, b_in, wout, b_out, fg, s_in,
    normed, normed_t, pre, slope, dhid, tmean, pooled_f, part64, tm64,
    tflat, tp, tj, trow, c1b, st_row, sp, sj, dref, da, dmsg, db, dbf,
    px, pin, pout16, pall, zmsg, dzr, dzm, dzf,
    own, sib, coreb, xs, xb, xm, xn, totf, zs, zb,
    s_tq, r_tq, s_tz, r_tz, s_c1, r_c1, s_px, r_px, s_cz, r_cz, s_cp, r_cp,
    s_da, r_da, s_db, r_db, s_pz, r_pz, s_pc, r_pc, s_dz, r_dz, s_df, r_df,
    s_co, r_co, s_x, r_x, s_xm, r_xm, s_z, r_z,
):
    d = lax.axis_index("dp")
    f = lax.axis_index("fsdp")
    xl = div(d, 2 * NZ)
    z = rem(div(d, 2), NZ)
    c = rem(d, 2)
    q = xl * 2 + c
    p = q * NF + f

    def dev(xx, zz, cc, ff):
        return ((xx * NZ + zz) * 2 + cc, ff)

    qs = [rem(q + k, 4) for k in range(4)]
    fs = [rem(f + k, NF) for k in range(NF)]
    ds = [(div(v, 2) * NZ + z) * 2 + rem(v, 2) for v in qs]
    near = [(0, kf) for kf in (3, 5, 4, 7, 1, 6, 2)]
    others = [(kq, kf) for kq in (2, 3, 1) for kf in (3, 5, 4, 7, 1, 6, 2, 0)]
    plane = near + others
    far_z = [NZ // 2 + (m + 1) // 2 * (1 - 2 * (m % 2)) for m in range(NZ - 1)]

    def copy(src, dst, ss, rs, to):
        return pltpu.make_async_remote_copy(
            src_ref=src, dst_ref=dst, send_sem=ss, recv_sem=rs, device_id=to, device_id_type=MESH
        )

    def each(lo, hi, fn):
        def step(k, carry):
            fn(k)
            return carry

        lax.fori_loop(lo, hi, step, 0)

    def along_z(fn):
        for k in far_z:
            fn(k)

    def load(n, src, dst):
        return pltpu.make_async_copy(src, dst, s_in.at[n])

    def load_tok(i):
        rows = pl.ds(pl.multiple_of(i * 256, 256), 256)
        return load(i, tok_h.at[rows], tok.at[rows])

    loads = [
        load(4 + n, src, dst)
        for n, (src, dst) in enumerate(
            [
                (tea_h, tea), (ng_h, ng), (win_h, win), (b_in_h, b_in),
                (wout_h, wout), (b_out_h, b_out), (fg_h, fg),
            ]
        )
    ]
    loads[0].start()
    loads[1].start()
    load_tok(0).start()
    loads[2].start()
    loads[3].start()
    each(1, 4, lambda i: load_tok(i).start())
    for item in loads[4:]:
        item.start()

    barrier = pltpu.get_barrier_semaphore()

    for k in far_z:
        pl.semaphore_signal(
            barrier, inc=1, device_id=dev(xl, rem(z + k, NZ), c, f), device_id_type=MESH
        )
    for kq, kf in plane:
        pl.semaphore_signal(barrier, inc=1, device_id=(ds[kq], fs[kf]), device_id_type=MESH)

    loads[0].wait()
    teacher = tea[...].astype(F32)
    t_norm = jnp.sqrt(jnp.sum(teacher * teacher, axis=-1, keepdims=True) + 1e-06)
    target = teacher / t_norm
    for a in range(16):
        for b in range(3):
            lo = 384 * a + 128 * b
            tflat[b, pl.ds(a, 8, stride=16), :] = target[:, lo : lo + 128]
    tp[q] = jnp.concatenate([tflat[b] for b in range(3)], axis=1).astype(BF16)
    own_rows = pl.ds(pl.multiple_of(f * 16, 16), 16)
    own_target = jnp.concatenate([tflat[b, own_rows, :] for b in range(3)], axis=1).astype(BF16)
    trow[...] = own_target
    tj[z] = own_target

    for item in loads[1:4]:
        item.wait()
    gain = ng[...]
    bias = b_in[...]

    def normalise(i):
        rows = slice(256 * i, 256 * i + 256)
        x = tok[rows, :].astype(F32)
        for n in range(2):
            tmean[2 * i + n : 2 * i + n + 1, :] = jnp.sum(
                x[128 * n : 128 * n + 128], axis=0, keepdims=True
            ) * (1.0 / PER_IMAGE)
        centered = x - jnp.mean(x, axis=-1, keepdims=True)
        inv = lax.rsqrt(jnp.mean(centered * centered, axis=-1, keepdims=True) + 1e-05)
        normed[rows, :] = (centered * inv * gain).astype(BF16)

    def activate(i):
        rows = slice(256 * i, 256 * i + 256)
        act = dot(normed[rows, :], win[...]) + bias
        pre[rows, :] = act
        g = 0.5 * act * (1.0 + gelu_parts(act))
        for n in range(2):
            pooled_f[2 * i + n : 2 * i + n + 1, :] = jnp.sum(
                g[128 * n : 128 * n + 128], axis=0, keepdims=True
            ) * (1.0 / PER_IMAGE)

    load_tok(0).wait()
    normalise(0)
    for i in range(2):
        load_tok(i + 1).wait()
        activate(i)
        normalise(i + 1)
    load_tok(3).wait()
    activate(2)
    normalise(3)
    activate(3)
    for item in loads[4:]:
        item.wait()
    pooled_b = pooled_f[...].astype(BF16)
    partial = dot_last(pooled_b, wout[...])
    mean_tok = tmean[...]
    for a in range(8):
        part64[pl.ds(a, 8, stride=8), :] = partial[:, 128 * a : 128 * a + 128]
        tm64[pl.ds(a, 8, stride=8), :] = mean_tok[:, 128 * a : 128 * a + 128]

    def c1_copy(k):
        ff = rem(f + k, NF)
        return copy(
            part64.at[pl.ds(pl.multiple_of(ff * 8, 8), 8)],
            c1b.at[f], s_c1, r_c1, (d, ff),
        )

    pl.semaphore_wait(barrier, NP - 1 + NZ - 1)
    def tq_copy(k):
        qq = rem(q + k, 4)
        return copy(
            tp.at[q], tp.at[q], s_tq, r_tq, dev(div(qq, 2), z, rem(qq, 2), f)
        )

    def tz_copy(k):
        return copy(trow, tj.at[z], s_tz, r_tz, dev(xl, rem(z + k, NZ), c, f))

    each(1, NF, lambda k: c1_copy(k).start())
    along_z(lambda k: tz_copy(k).start())
    c1b[f] = part64[pl.ds(pl.multiple_of(f * 8, 8), 8), :]
    px[...] = pooled_b.astype(F32)

    def px_copy():
        return copy(px, pin, s_px, r_px, dev(1 - xl, z, c, f))

    px_copy().start()
    each(1, 4, lambda k: tq_copy(k).start())

    def slopes(i):
        rows = pl.ds(pl.multiple_of(i * 128, 128), 128)
        v = pre[rows, :]
        t = gelu_parts(v)
        slope[rows, :] = 0.5 * (1.0 + t) + 0.5 * v * (1.0 - t * t) * 0.7978845608 * (
            1.0 + 3.0 * 0.044715 * v * v
        )

    each(0, 8, slopes)

    def wait_from(dst, ss, rs):
        copy(dst, dst, ss, rs, (d, f)).wait_recv()

    def sent(src, ss, rs):
        copy(src, src, ss, rs, (d, f)).wait_send()

    wait_from(c1b.at[0 : NF - 1], s_c1, r_c1)
    embedding = jnp.sum(c1b[...], axis=0) + tm64[pl.ds(pl.multiple_of(f * 8, 8), 8), :] + b_out[...]
    final_gain = fg[...]

    def total(v):
        return jnp.sum(jnp.sum(v, axis=1, keepdims=True), axis=0, keepdims=True)

    cent = embedding - total(embedding) * (1.0 / D)
    inv_std = lax.rsqrt(total(cent * cent) * (1.0 / D) + 1e-05)
    n_emb = cent * inv_std
    unit = n_emb * final_gain
    unit_norm = jnp.sqrt(total(unit * unit) + 1e-06)
    unit_dir = unit / unit_norm
    student = unit_dir.astype(BF16).astype(F32)
    st_row[...] = student

    def cz_copy(k):
        return copy(st_row, sj.at[z], s_cz, r_cz, dev(xl, rem(z + k, NZ), c, f))

    def cp_copy(k):
        return copy(st_row, sp.at[p], s_cp, r_cp, (ds[k[0]], fs[k[1]]))

    along_z(lambda k: cz_copy(k).start())
    for k in plane:
        cp_copy(k).start()
    sj[z] = student
    sp[p] = student

    wait_from(tp.at[0:3], s_tq, r_tq)
    wait_from(tj.at[0 : NZ - 1], s_tz, r_tz)
    tx = dot_last(tp[...].reshape(NP * 16, 384), tj[...].reshape(NZ * 16, 384))
    same = (iota(tx.shape, 0) % 16) == (iota(tx.shape, 1) % 16)
    tx = jnp.sum(jnp.where(same, tx, 0.0).reshape(NP, 16, NZ * 16), axis=1)
    spread = ((iota((NZ * 16, 128), 0) // 16) == (iota((NZ * 16, 128), 1) // 8)).astype(BF16)
    gram_t = dot_exact(tx, spread)

    def pz_copy(k):
        return copy(
            pout16, pall.at[c, z], s_pz, r_pz, dev(xl, rem(z + k, NZ), c, f)
        )

    wait_from(pin, s_px, r_px)
    mine, other = px[...], pin[...]
    first = xl == 0
    block16 = jnp.concatenate(
        [jnp.where(first, mine, other), jnp.where(first, other, mine)], axis=0
    ).astype(BF16)
    pout16[...] = block16
    pall[c, z] = block16

    for i in range(4):
        turned_cols = slice(256 * i, 256 * i + 256)
        normed_t[turned_cols, :] = normed[:, turned_cols].T

    wait_from(sp.at[0 : NP - 1], s_cp, r_cp)
    wait_from(sj.at[0 : NZ - 1], s_cz, r_cz)
    s_plane = sp[...].reshape(NP * 8, 128).astype(BF16)
    s_other = sj[...].reshape(NZ * 8, 128).astype(BF16)
    sx = dot_last(s_plane, s_other)
    diag = (iota(sx.shape, 0) % 8) == (iota(sx.shape, 1) % 8)
    sx = jnp.sum(jnp.where(diag, sx, 0.0).reshape(NP, 8, 128), axis=1)
    group = ((iota((128, 128), 0) // 8) == (iota((128, 128), 1) // 8)).astype(BF16)
    resid = dot_exact(sx, group) - gram_t
    share = total(resid * resid) * 0.125
    wide = jnp.broadcast_to(resid[:, None, :], (NP, 8, 128)).reshape(NP * 8, 128)
    wide = jnp.where(diag, wide, 0.0).astype(BF16)
    dref[...] = dot(wide, s_other).reshape(NP, 8, 128)

    def da_copy(k):
        return copy(
            dref.at[qs[k[0]] * NF + fs[k[1]]], da.at[p], s_da, r_da, (ds[k[0]], fs[k[1]])
        )

    for k in plane:
        da_copy(k).start()
    da[p] = dref[p]
    along_z(lambda k: pz_copy(k).start())

    wait_from(da.at[0 : NP - 1], s_da, r_da)
    dstudent = (LOSS_SCALE * 4.0 / IMAGES) * jnp.sum(da[...], axis=0)
    dunit = (dstudent - unit_dir * total(unit_dir * dstudent)) / unit_norm
    gain_grad = dunit * final_gain
    dembed = inv_std * (
        gain_grad - total(gain_grad) * (1.0 / D) - n_emb * (total(gain_grad * n_emb) * (1.0 / D))
    )
    high = share.astype(BF16).astype(F32)
    mid = (share - high).astype(BF16).astype(F32)
    last = share - high - mid
    row = iota((8, 128), 0)
    terms = jnp.where(row == 0, high, jnp.where(row == 1, mid, jnp.where(row == 2, last, 0.0)))
    message = jnp.concatenate([dembed, terms], axis=0).astype(BF16)
    dmsg[...] = message

    def rows16(pp):
        return pl.ds(pl.multiple_of(pp * 16, 16), 16)

    def db_copy(k, part):
        return copy(
            dmsg, db.at[rows16(p)], s_db.at[part], r_db.at[part], (ds[k[0]], fs[k[1]])
        )

    for k in near:
        db_copy(k, 0).start()
    for k in others:
        db_copy(k, 1).start()
    db[rows16(p), :] = message

    wait_from(db.at[0 : (NF - 1) * 16], s_db.at[0], r_db.at[0])
    own_rows = pl.ds(pl.multiple_of(q * (NF * 16), NF * 16), NF * 16)
    dbf[own_rows, :] = db[own_rows, :].astype(F32)
    block = jnp.concatenate(
        [dbf[pl.ds(q * (NF * 16) + a, 8, stride=16), :] for a in range(8)], axis=1
    ).astype(BF16)
    tmean[:, :HID] = dot(block, wout[...]) * (1.0 / PER_IMAGE)

    def hidden(i):
        rows = pl.ds(pl.multiple_of(i * PER_IMAGE, PER_IMAGE), PER_IMAGE)
        dhid[rows, :] = (tmean[pl.ds(i, 1), :HID] * slope[rows, :]).astype(BF16)

    each(0, 8, hidden)

    low = c == 0
    s_bit = rem(z, 2)
    w = div(z, 2)

    def half(h):
        return rem(div(w, 4) + 1 + h, 2)

    def co_copy(j):
        return copy(sib.at[j], coreb.at[j], s_co, r_co.at[j], dev(xl, z, 1 - c, f))

    step = 1 - 2 * s_bit

    def near_copy(t, h):
        xx = xl if t >= 3 else 1 - xl
        zz = z if t == 2 else rem(z + NZ + (step if t in (0, 3) else -step), NZ)
        if t == 2:
            return copy(xm.at[h], xn.at[h], s_xm, r_xm.at[h], dev(xx, zz, c, f))
        n = t if t < 2 else t - 1
        return copy(xs.at[n, h], xb.at[h, n], s_x, r_x.at[h], dev(xx, zz, c, f))

    def core_sum(j, bit):
        return own[j, bit] + coreb[j, bit].astype(F32)

    def near_send(j):
        wait_from(coreb.at[j], s_co, r_co.at[j])
        h = half(j % 2)
        across = core_sum(j, 1 - s_bit).astype(BF16)
        first = 0 if j < 2 else 2
        for n in range(2):
            xs[first + n, h] = across[:, :, 256 * n : 256 * n + 256]
        if j < 2:
            near_copy(0, h).start()
            near_copy(1, h).start()
            xm[h] = core_sum(j, s_bit).astype(BF16)
            near_copy(2, h).start()
        else:
            near_copy(3, h).start()
            near_copy(4, h).start()

    octave = div(z, NF)
    turning = rem(z, NF) == f

    def dz_copy(k):
        zz = rem(z + k, NZ)
        return copy(zmsg.at[zz], dzr.at[octave], s_dz, r_dz, dev(xl, zz, c, f))

    def turn():
        wait_from(db.at[0 : (NP - NF) * 16], s_db.at[1], r_db.at[1])

        @pl.when(turning)
        def _():
            dbf[...] = db[...].astype(F32)
            loss_plane = jnp.zeros((8, 128), F32)
            for pp in range(NP):
                loss_plane = loss_plane + dbf[pp * 16 + 8 : pp * 16 + 16, :]
            loss_plane = jnp.sum(loss_plane, axis=0, keepdims=True)
            flat = jnp.concatenate(
                [dbf[pl.ds(xl * 4 + a, NP, stride=16), :] for a in range(4)], axis=1
            ).astype(BF16)
            image = iota((NP, 128), 0)
            lane = octave * 32 + ((image // 8) % 2) * 16 + (image // 16) * 8 + image % 8
            place = (lane == iota((NP, 128), 1)).astype(BF16)
            turned = dot_first(flat, place).reshape(NZ, 2, 16, 128)
            turned = jnp.where(low, turned[:, 0], turned[:, 1])
            high = loss_plane.astype(BF16).astype(F32)
            mid = (loss_plane - high).astype(BF16).astype(F32)
            last = loss_plane - high - mid
            at = iota((1, 128), 1) - (64 + 4 * octave)
            extra = jnp.where(
                at == 0, high, jnp.where(at == 1, mid, jnp.where(at == 2, last, 0.0))
            )
            zmsg[...] = (turned + extra[None]).astype(BF16)
            dzr[octave] = zmsg[z]
            along_z(lambda k: dz_copy(k).start())

    for j in range(4):
        side = (1 - xl) if j < 2 else xl
        cols = pl.ds(pl.multiple_of(side * 512 + half(j % 2) * 256, 256), 256)
        term = dot(normed_t[cols, :], dhid[...]).reshape(4, 2, 2, 16, HID)
        for bit in range(2):
            mine_t, other_t = term[:, bit, 0], term[:, bit, 1]
            own[j, bit] = jnp.where(low, mine_t, other_t)
            sib[j, bit] = jnp.where(low, other_t, mine_t).astype(BF16)
        co_copy(j).start()
        if j >= 1:
            near_send(j - 1)
        if j == 2:
            turn()

    near_send(3)

    def z_copy(k):
        ww = rem(w + k, NW)
        return copy(zs.at[ww], zb.at[w], s_z, r_z, dev(xl, 2 * ww + s_bit, c, f))

    zb[w] = jnp.zeros((16, HID), BF16)
    for h in range(2):
        merged = core_sum(2 + h, s_bit)
        hh = half(h)
        wait_from(xn.at[hh], s_xm, r_xm.at[hh])
        merged = merged + xn[hh].astype(F32)
        wait_from(xb.at[hh], s_x, r_x.at[hh])
        sides = [xb[hh, n].astype(F32) + xb[hh, 2 + n].astype(F32) for n in range(2)]
        merged = merged + jnp.concatenate(sides, axis=2)
        blocks = pl.ds(hh * 4, 4)
        totf[blocks] = merged
        zs[blocks] = merged.astype(BF16)
        for k in (4, 3, 5, 2, 6, 1, 7):

            @pl.when(div(rem(w + k, NW), 4) == hh)
            def _():
                z_copy(k).start()

    @pl.when(turning)
    def _():
        wait_from(dzr.at[1 - octave], s_dz, r_dz)

    @pl.when(jnp.logical_not(turning))
    def _():
        wait_from(dzr, s_dz, r_dz)

    pair = (dzr[0].astype(F32) + dzr[1].astype(F32)).astype(BF16)
    dzm[...] = pair
    dzf[f] = pair

    def df_copy(k):
        return copy(dzm, dzf.at[f], s_df, r_df, (d, fs[k]))

    for _, kf in near:
        df_copy(kf).start()

    def pc_copy():
        return copy(pall.at[c], pall.at[c], s_pc, r_pc, dev(xl, z, 1 - c, f))

    wait_from(pall.at[c, 0 : NZ - 1], s_pz, r_pz)
    pc_copy().start()

    wait_from(dzf.at[0 : NF - 1], s_df, r_df)
    wait_from(pall.at[1 - c], s_pc, r_pc)
    acc = jnp.zeros((16, HID), F32)
    loss = jnp.zeros((16, 128), F32)
    for g in range(NF):
        left = dzf[g]
        loss = loss + left.astype(F32)
        right = jnp.concatenate([pall[cc, zz] for zz in (g, g + NF) for cc in range(2)], axis=0)
        acc = acc + dot(left[:, :64], right)
    out_ref[16:32, :] = acc.astype(BF16)
    loss = jnp.sum(jnp.where(iota((16, 128), 1) >= 64, loss, 0.0), axis=1, keepdims=True)
    loss_ref[...] = jnp.broadcast_to(loss[:8], (8, 128)) * (1.0 / IMAGES)

    sent(tp.at[0:3], s_tq, r_tq)
    sent(tj.at[0 : NZ - 1], s_tz, r_tz)
    sent(c1b.at[0 : NF - 1], s_c1, r_c1)
    sent(px, s_px, r_px)
    sent(sj.at[0 : NZ - 1], s_cz, r_cz)
    sent(sp.at[0 : NP - 1], s_cp, r_cp)
    sent(da.at[0 : NP - 1], s_da, r_da)
    sent(pall.at[c, 0 : NZ - 1], s_pz, r_pz)
    sent(db.at[0 : (NF - 1) * 16], s_db.at[0], r_db.at[0])
    sent(db.at[0 : (NP - NF) * 16], s_db.at[1], r_db.at[1])
    sent(dzf.at[0 : NF - 1], s_df, r_df)

    @pl.when(turning)
    def _():
        sent(zmsg.at[0 : NZ - 1], s_dz, r_dz)

    sent(sib, s_co, r_co.at[0])
    sent(xs, s_x, r_x.at[0])
    sent(xm, s_xm, r_xm.at[0])
    sent(pall.at[c], s_pc, r_pc)

    wait_from(zb.at[0 : NW - 1], s_z, r_z)
    out_ref[0:16, :] = (totf[w] + jnp.sum(zb[...].astype(F32), axis=0)).astype(BF16)
    sent(zb.at[0 : NW - 1], s_z, r_z)


def body(tokens, teacher, norm_gain, w_in, b_in, w_out, b_out, final_gain):
    vmem = pl.BlockSpec(memory_space=pltpu.VMEM)
    one, two, four = (
        pltpu.SemaphoreType.DMA, pltpu.SemaphoreType.DMA((2,)), pltpu.SemaphoreType.DMA((4,))
    )
    sems = [one, one] * 7 + [two, two] + [one, one] * 4 + [one, four] + [one, two] * 2 + [one, one]
    packed, loss = pl.pallas_call(
        kernel,
        name="gram_step",
        out_shape=(
            jax.ShapeDtypeStruct((32, HID), BF16),
            jax.ShapeDtypeStruct((8, 128), F32),
        ),
        in_specs=[pl.BlockSpec(memory_space=pl.ANY)] * 8,
        out_specs=(vmem, vmem),
        scratch_shapes=[
            pltpu.VMEM((1024, D), BF16),
            pltpu.VMEM((8, DT), BF16),
            pltpu.VMEM((1, D), F32),
            pltpu.VMEM((D, HID), BF16),
            pltpu.VMEM((1, HID), F32),
            pltpu.VMEM((D, HID), BF16),
            pltpu.VMEM((8, 128), F32),
            pltpu.VMEM((8, 128), F32),
            pltpu.SemaphoreType.DMA((11,)),
            pltpu.VMEM((1024, D), BF16),
            pltpu.VMEM((D, 1024), BF16),
            pltpu.VMEM((1024, HID), F32),
            pltpu.VMEM((1024, HID), F32),
            pltpu.VMEM((1024, HID), BF16),
            pltpu.VMEM((8, D), F32),
            pltpu.VMEM((8, HID), F32),
            pltpu.VMEM((64, 128), F32),
            pltpu.VMEM((64, 128), F32),
            pltpu.VMEM((3, 128, 128), F32),
            pltpu.VMEM((4, 128, 384), BF16),
            pltpu.VMEM((NZ, 16, 384), BF16),
            pltpu.VMEM((16, 384), BF16),
            pltpu.VMEM((NF, 8, 128), F32),
            pltpu.VMEM((8, 128), F32),
            pltpu.VMEM((NP, 8, 128), F32),
            pltpu.VMEM((NZ, 8, 128), F32),
            pltpu.VMEM((NP, 8, 128), F32),
            pltpu.VMEM((NP, 8, 128), F32),
            pltpu.VMEM((16, 128), BF16),
            pltpu.VMEM((NP * 16, 128), BF16),
            pltpu.VMEM((NP * 16, 128), F32),
            pltpu.VMEM((8, HID), F32),
            pltpu.VMEM((8, HID), F32),
            pltpu.VMEM((16, HID), BF16),
            pltpu.VMEM((2, NZ, 16, HID), BF16),
            pltpu.VMEM((NZ, 16, 128), BF16),
            pltpu.VMEM((2, 16, 128), BF16),
            pltpu.VMEM((16, 128), BF16),
            pltpu.VMEM((NF, 16, 128), BF16),
            pltpu.VMEM((4, 2, 4, 16, HID), F32),
            pltpu.VMEM((4, 2, 4, 16, HID), BF16),
            pltpu.VMEM((4, 2, 4, 16, HID), BF16),
            pltpu.VMEM((4, 2, 4, 16, HID // 2), BF16),
            pltpu.VMEM((2, 4, 4, 16, HID // 2), BF16),
            pltpu.VMEM((2, 4, 16, HID), BF16),
            pltpu.VMEM((2, 4, 16, HID), BF16),
            pltpu.VMEM((NW, 16, HID), F32),
            pltpu.VMEM((NW, 16, HID), BF16),
            pltpu.VMEM((NW, 16, HID), BF16),
        ]
        + sems,
        compiler_params=pltpu.CompilerParams(
            collective_id=0, has_side_effects=True, vmem_limit_bytes=56 << 20
        ),
        cost_estimate=pl.CostEstimate(
            flops=5_000_000_000, bytes_accessed=8_000_000, transcendentals=1_000_000
        ),
    )(
        tokens,
        teacher,
        norm_gain.reshape(1, D),
        w_in,
        b_in.reshape(1, HID),
        w_out,
        b_out.reshape(8, 128),
        final_gain.reshape(8, 128),
    )
    return loss[0, 0], packed[:16], packed[16:]


def solution(mesh):
    return jax.shard_map(
        body,
        mesh=mesh,
        in_specs=(
            P("dp", None),
            P("dp", None),
            P(),
            P(None, "fsdp"),
            P("fsdp"),
            P(None, "fsdp"),
            P(),
            P(),
        ),
        out_specs=(P(), P("dp", "fsdp"), P("dp", "fsdp")),
        check_vma=False,
    )
```

```python
import jax
import jax.numpy as jnp
from jax import lax
from jax.experimental import pallas as pl
from jax.experimental.pallas import tpu as pltpu
from jax.sharding import PartitionSpec as P

MESH = pl.DeviceIdType.MESH
F32 = jnp.float32
BF16 = jnp.bfloat16

NZ = 16
NF = 8
NW = 8
NP = 32
LOSS_SCALE = 4096.0
IMAGES = 512
PER_IMAGE = 128
D = 1024
DT = 6144
HID = 512


def dot(left, right):
    return jnp.dot(left, right, preferred_element_type=F32)


def dot_last(left, right):
    return lax.dot_general(left, right, (((1,), (1,)), ((), ())), preferred_element_type=F32)


def dot_first(left, right):
    return lax.dot_general(left, right, (((0,), (0,)), ((), ())), preferred_element_type=F32)


def dot_exact(values, ones):
    high = values.astype(BF16)
    rest = values - high.astype(F32)
    mid = rest.astype(BF16)
    low = (rest - mid.astype(F32)).astype(BF16)
    return dot(high, ones) + dot(mid, ones) + dot(low, ones)


def div(value, by):
    return lax.div(value, jnp.int32(by))


def rem(value, by):
    return lax.rem(value, jnp.int32(by))


def iota(shape, axis):
    return lax.broadcasted_iota(jnp.int32, shape, axis)


def gelu_parts(values):
    inner = 0.7978845608 * (values + 0.044715 * values * values * values)
    return jnp.tanh(inner)


def kernel(
    tok_h, tea_h, ng_h, win_h, b_in_h, wout_h, b_out_h, fg_h,
    out_ref, loss_ref,
    tok, tea, ng, win, b_in, wout, b_out, fg, s_in,
    normed, normed_t, pre, slope, dhid, tmean, pooled_f, part64, tm64,
    tflat, tp, tj, trow, c1b, st_row, sp, sj, dref, da, dmsg, db, dbf,
    px, pin, pout16, pall, zmsg, dzr, dzm, dzf,
    own, sib, coreb, xs, xb, xm, xn, totf, zs, zb,
    s_tq, r_tq, s_tz, r_tz, s_c1, r_c1, s_px, r_px, s_cz, r_cz, s_cp, r_cp,
    s_da, r_da, s_db, r_db, s_pz, r_pz, s_pc, r_pc, s_dz, r_dz, s_df, r_df,
    s_co, r_co, s_x, r_x, s_xm, r_xm, s_z, r_z, s_far,
):
    d = lax.axis_index("dp")
    f = lax.axis_index("fsdp")
    xl = div(d, 2 * NZ)
    z = rem(div(d, 2), NZ)
    c = rem(d, 2)
    q = xl * 2 + c
    p = q * NF + f

    def dev(xx, zz, cc, ff):
        return ((xx * NZ + zz) * 2 + cc, ff)

    qs = [rem(q + k, 4) for k in range(4)]
    fs = [rem(f + k, NF) for k in range(NF)]
    ds = [(div(v, 2) * NZ + z) * 2 + rem(v, 2) for v in qs]
    near = [(0, kf) for kf in (3, 5, 4, 7, 1, 6, 2)]
    others = [(kq, kf) for kq in (2, 3, 1) for kf in (3, 5, 4, 7, 1, 6, 2, 0)]
    plane = near + others
    far_z = [NZ // 2 + (m + 1) // 2 * (1 - 2 * (m % 2)) for m in range(NZ - 1)]
    step_z = NZ // 4
    close_z = [k for k in far_z if min(k, NZ - k) <= step_z]
    away_z = [k for k in far_z if k not in close_z]

    def copy(src, dst, ss, rs, to):
        return pltpu.make_async_remote_copy(
            src_ref=src, dst_ref=dst, send_sem=ss, recv_sem=rs, device_id=to, device_id_type=MESH
        )

    def each(lo, hi, fn):
        def step(k, carry):
            fn(k)
            return carry

        lax.fori_loop(lo, hi, step, 0)

    def along_z(fn, steps=far_z):
        for k in steps:
            fn(k)

    def load(n, src, dst):
        return pltpu.make_async_copy(src, dst, s_in.at[n])

    def load_tok(i):
        rows = pl.ds(pl.multiple_of(i * 256, 256), 256)
        return load(i, tok_h.at[rows], tok.at[rows])

    loads = [
        load(4 + n, src, dst)
        for n, (src, dst) in enumerate(
            [
                (tea_h, tea), (ng_h, ng), (win_h, win), (b_in_h, b_in),
                (wout_h, wout), (b_out_h, b_out), (fg_h, fg),
            ]
        )
    ]
    loads[0].start()
    loads[1].start()
    load_tok(0).start()
    loads[2].start()
    loads[3].start()
    each(1, 4, lambda i: load_tok(i).start())
    for item in loads[4:]:
        item.start()

    barrier = pltpu.get_barrier_semaphore()

    for k in close_z:
        pl.semaphore_signal(
            barrier, inc=1, device_id=dev(xl, rem(z + k, NZ), c, f), device_id_type=MESH
        )
    for kq, kf in plane:
        pl.semaphore_signal(barrier, inc=1, device_id=(ds[kq], fs[kf]), device_id_type=MESH)

    loads[0].wait()
    teacher = tea[...].astype(F32)
    t_norm = jnp.sqrt(jnp.sum(teacher * teacher, axis=-1, keepdims=True) + 1e-06)
    target = teacher / t_norm
    for a in range(16):
        for b in range(3):
            lo = 384 * a + 128 * b
            tflat[b, pl.ds(a, 8, stride=16), :] = target[:, lo : lo + 128]
    tp[q] = jnp.concatenate([tflat[b] for b in range(3)], axis=1).astype(BF16)
    own_rows = pl.ds(pl.multiple_of(f * 16, 16), 16)
    own_target = jnp.concatenate([tflat[b, own_rows, :] for b in range(3)], axis=1).astype(BF16)
    trow[...] = own_target
    tj[z] = own_target

    for item in loads[1:4]:
        item.wait()
    gain = ng[...]
    bias = b_in[...]

    def normalise(i):
        rows = slice(256 * i, 256 * i + 256)
        x = tok[rows, :].astype(F32)
        for n in range(2):
            tmean[2 * i + n : 2 * i + n + 1, :] = jnp.sum(
                x[128 * n : 128 * n + 128], axis=0, keepdims=True
            ) * (1.0 / PER_IMAGE)
        centered = x - jnp.mean(x, axis=-1, keepdims=True)
        inv = lax.rsqrt(jnp.mean(centered * centered, axis=-1, keepdims=True) + 1e-05)
        normed[rows, :] = (centered * inv * gain).astype(BF16)

    def activate(i):
        rows = slice(256 * i, 256 * i + 256)
        act = dot(normed[rows, :], win[...]) + bias
        pre[rows, :] = act
        g = 0.5 * act * (1.0 + gelu_parts(act))
        for n in range(2):
            pooled_f[2 * i + n : 2 * i + n + 1, :] = jnp.sum(
                g[128 * n : 128 * n + 128], axis=0, keepdims=True
            ) * (1.0 / PER_IMAGE)

    load_tok(0).wait()
    normalise(0)
    for i in range(2):
        load_tok(i + 1).wait()
        activate(i)
        normalise(i + 1)
    def tz_copy(k):
        return copy(trow, tj.at[z], s_tz, r_tz, dev(xl, rem(z + k, NZ), c, f))

    pl.semaphore_wait(barrier, NP - 1 + len(close_z))
    for k in (step_z, NZ - step_z):
        pl.semaphore_signal(
            s_far, inc=1, device_id=dev(xl, rem(z + k, NZ), c, f), device_id_type=MESH
        )
    along_z(lambda k: tz_copy(k).start(), close_z)

    load_tok(3).wait()
    activate(2)
    normalise(3)
    activate(3)
    for item in loads[4:]:
        item.wait()
    pooled_b = pooled_f[...].astype(BF16)
    partial = dot_last(pooled_b, wout[...])
    mean_tok = tmean[...]
    for a in range(8):
        part64[pl.ds(a, 8, stride=8), :] = partial[:, 128 * a : 128 * a + 128]
        tm64[pl.ds(a, 8, stride=8), :] = mean_tok[:, 128 * a : 128 * a + 128]

    def c1_copy(k):
        ff = rem(f + k, NF)
        return copy(
            part64.at[pl.ds(pl.multiple_of(ff * 8, 8), 8)],
            c1b.at[f], s_c1, r_c1, (d, ff),
        )

    def tq_copy(k):
        qq = rem(q + k, 4)
        return copy(
            tp.at[q], tp.at[q], s_tq, r_tq, dev(div(qq, 2), z, rem(qq, 2), f)
        )


    each(1, NF, lambda k: c1_copy(k).start())
    c1b[f] = part64[pl.ds(pl.multiple_of(f * 8, 8), 8), :]
    px[...] = pooled_b.astype(F32)

    def px_copy():
        return copy(px, pin, s_px, r_px, dev(1 - xl, z, c, f))

    px_copy().start()
    each(1, 4, lambda k: tq_copy(k).start())

    def slopes(i):
        rows = pl.ds(pl.multiple_of(i * 128, 128), 128)
        v = pre[rows, :]
        t = gelu_parts(v)
        slope[rows, :] = 0.5 * (1.0 + t) + 0.5 * v * (1.0 - t * t) * 0.7978845608 * (
            1.0 + 3.0 * 0.044715 * v * v
        )

    each(0, 8, slopes)

    def wait_from(dst, ss, rs):
        copy(dst, dst, ss, rs, (d, f)).wait_recv()

    def sent(src, ss, rs):
        copy(src, src, ss, rs, (d, f)).wait_send()

    pl.semaphore_wait(s_far, 2)
    along_z(lambda k: tz_copy(k).start(), away_z)

    wait_from(c1b.at[0 : NF - 1], s_c1, r_c1)
    embedding = jnp.sum(c1b[...], axis=0) + tm64[pl.ds(pl.multiple_of(f * 8, 8), 8), :] + b_out[...]
    final_gain = fg[...]

    def total(v):
        return jnp.sum(jnp.sum(v, axis=1, keepdims=True), axis=0, keepdims=True)

    cent = embedding - total(embedding) * (1.0 / D)
    inv_std = lax.rsqrt(total(cent * cent) * (1.0 / D) + 1e-05)
    n_emb = cent * inv_std
    unit = n_emb * final_gain
    unit_norm = jnp.sqrt(total(unit * unit) + 1e-06)
    unit_dir = unit / unit_norm
    student = unit_dir.astype(BF16).astype(F32)
    st_row[...] = student

    def cz_copy(k):
        return copy(st_row, sj.at[z], s_cz, r_cz, dev(xl, rem(z + k, NZ), c, f))

    def cp_copy(k):
        return copy(st_row, sp.at[p], s_cp, r_cp, (ds[k[0]], fs[k[1]]))

    along_z(lambda k: cz_copy(k).start())
    for k in plane:
        cp_copy(k).start()
    sj[z] = student
    sp[p] = student

    for i in range(4):
        turned_cols = slice(256 * i, 256 * i + 256)
        normed_t[turned_cols, :] = normed[:, turned_cols].T

    wait_from(tp.at[0:3], s_tq, r_tq)
    wait_from(tj.at[0 : NZ - 1], s_tz, r_tz)
    tx = dot_last(tp[...].reshape(NP * 16, 384), tj[...].reshape(NZ * 16, 384))
    same = (iota(tx.shape, 0) % 16) == (iota(tx.shape, 1) % 16)
    tx = jnp.sum(jnp.where(same, tx, 0.0).reshape(NP, 16, NZ * 16), axis=1)
    spread = ((iota((NZ * 16, 128), 0) // 16) == (iota((NZ * 16, 128), 1) // 8)).astype(BF16)
    gram_t = dot_exact(tx, spread)

    def pz_copy(k):
        return copy(
            pout16, pall.at[c, z], s_pz, r_pz, dev(xl, rem(z + k, NZ), c, f)
        )

    wait_from(pin, s_px, r_px)
    mine, other = px[...], pin[...]
    first = xl == 0
    block16 = jnp.concatenate(
        [jnp.where(first, mine, other), jnp.where(first, other, mine)], axis=0
    ).astype(BF16)
    pout16[...] = block16
    pall[c, z] = block16

    wait_from(sp.at[0 : NP - 1], s_cp, r_cp)
    wait_from(sj.at[0 : NZ - 1], s_cz, r_cz)
    s_plane = sp[...].reshape(NP * 8, 128).astype(BF16)
    s_other = sj[...].reshape(NZ * 8, 128).astype(BF16)
    sx = dot_last(s_plane, s_other)
    diag = (iota(sx.shape, 0) % 8) == (iota(sx.shape, 1) % 8)
    sx = jnp.sum(jnp.where(diag, sx, 0.0).reshape(NP, 8, 128), axis=1)
    group = ((iota((128, 128), 0) // 8) == (iota((128, 128), 1) // 8)).astype(BF16)
    resid = dot_exact(sx, group) - gram_t
    share = total(resid * resid) * 0.125
    wide = jnp.broadcast_to(resid[:, None, :], (NP, 8, 128)).reshape(NP * 8, 128)
    wide = jnp.where(diag, wide, 0.0).astype(BF16)
    dref[...] = dot(wide, s_other).reshape(NP, 8, 128)

    def da_copy(k):
        return copy(
            dref.at[qs[k[0]] * NF + fs[k[1]]], da.at[p], s_da, r_da, (ds[k[0]], fs[k[1]])
        )

    for k in plane:
        da_copy(k).start()
    da[p] = dref[p]
    along_z(lambda k: pz_copy(k).start())

    wait_from(da.at[0 : NP - 1], s_da, r_da)
    dstudent = (LOSS_SCALE * 4.0 / IMAGES) * jnp.sum(da[...], axis=0)
    dunit = (dstudent - unit_dir * total(unit_dir * dstudent)) / unit_norm
    gain_grad = dunit * final_gain
    dembed = inv_std * (
        gain_grad - total(gain_grad) * (1.0 / D) - n_emb * (total(gain_grad * n_emb) * (1.0 / D))
    )
    high = share.astype(BF16).astype(F32)
    mid = (share - high).astype(BF16).astype(F32)
    last = share - high - mid
    row = iota((8, 128), 0)
    terms = jnp.where(row == 0, high, jnp.where(row == 1, mid, jnp.where(row == 2, last, 0.0)))
    message = jnp.concatenate([dembed, terms], axis=0).astype(BF16)
    dmsg[...] = message

    def rows16(pp):
        return pl.ds(pl.multiple_of(pp * 16, 16), 16)

    def db_copy(k, part):
        return copy(
            dmsg, db.at[rows16(p)], s_db.at[part], r_db.at[part], (ds[k[0]], fs[k[1]])
        )

    for k in near:
        db_copy(k, 0).start()
    for k in others:
        db_copy(k, 1).start()
    db[rows16(p), :] = message

    wait_from(db.at[0 : (NF - 1) * 16], s_db.at[0], r_db.at[0])
    own_rows = pl.ds(pl.multiple_of(q * (NF * 16), NF * 16), NF * 16)
    dbf[own_rows, :] = db[own_rows, :].astype(F32)
    block = jnp.concatenate(
        [dbf[pl.ds(q * (NF * 16) + a, 8, stride=16), :] for a in range(8)], axis=1
    ).astype(BF16)
    tmean[:, :HID] = dot(block, wout[...]) * (1.0 / PER_IMAGE)

    def hidden(i):
        rows = pl.ds(pl.multiple_of(i * PER_IMAGE, PER_IMAGE), PER_IMAGE)
        dhid[rows, :] = (tmean[pl.ds(i, 1), :HID] * slope[rows, :]).astype(BF16)

    each(0, 8, hidden)

    low = c == 0
    s_bit = rem(z, 2)
    w = div(z, 2)

    def half(h):
        return rem(div(w, 4) + 1 + h, 2)

    def co_copy(j):
        return copy(sib.at[j], coreb.at[j], s_co, r_co.at[j], dev(xl, z, 1 - c, f))

    step = 1 - 2 * s_bit

    def near_copy(t, quarter):
        xx = xl if t >= 3 else 1 - xl
        zz = z if t == 2 else rem(z + NZ + (step if t in (0, 3) else -step), NZ)
        to = dev(xx, zz, c, f)
        if t == 2:
            return copy(xm.at[quarter], xn.at[quarter], s_xm, r_xm.at[quarter], to)
        n = t if t < 2 else t - 1
        return copy(xs.at[n, quarter], xb.at[quarter, n], s_x, r_x.at[quarter], to)

    def core_sum(j, bit):
        return own[j, bit] + coreb[j, bit].astype(F32)

    def near_send(j):
        wait_from(coreb.at[j], s_co, r_co.at[j])
        across = core_sum(j, 1 - s_bit).astype(BF16)
        along = core_sum(j, s_bit).astype(BF16) if j < 2 else None
        for u in range(2):
            quarter = half(j % 2) * 2 + u
            for n in range(2):
                t = n if j < 2 else 3 + n
                xs[t - t // 3, quarter] = across[2 * u : 2 * u + 2, :, 256 * n : 256 * n + 256]
                near_copy(t, quarter).start()
            if j < 2:
                xm[quarter] = along[2 * u : 2 * u + 2]
                near_copy(2, quarter).start()

    octave = div(z, NF)
    turning = rem(z, NF) == f

    def dz_copy(k):
        zz = rem(z + k, NZ)
        return copy(zmsg.at[zz], dzr.at[octave], s_dz, r_dz, dev(xl, zz, c, f))

    def turn():
        wait_from(db.at[0 : (NP - NF) * 16], s_db.at[1], r_db.at[1])

        @pl.when(turning)
        def _():
            dbf[...] = db[...].astype(F32)
            loss_plane = jnp.zeros((8, 128), F32)
            for pp in range(NP):
                loss_plane = loss_plane + dbf[pp * 16 + 8 : pp * 16 + 16, :]
            loss_plane = jnp.sum(loss_plane, axis=0, keepdims=True)
            flat = jnp.concatenate(
                [dbf[pl.ds(xl * 4 + a, NP, stride=16), :] for a in range(4)], axis=1
            ).astype(BF16)
            image = iota((NP, 128), 0)
            lane = octave * 32 + ((image // 8) % 2) * 16 + (image // 16) * 8 + image % 8
            place = (lane == iota((NP, 128), 1)).astype(BF16)
            turned = dot_first(flat, place).reshape(NZ, 2, 16, 128)
            turned = jnp.where(low, turned[:, 0], turned[:, 1])
            high = loss_plane.astype(BF16).astype(F32)
            mid = (loss_plane - high).astype(BF16).astype(F32)
            last = loss_plane - high - mid
            at = iota((1, 128), 1) - (64 + 4 * octave)
            extra = jnp.where(
                at == 0, high, jnp.where(at == 1, mid, jnp.where(at == 2, last, 0.0))
            )
            zmsg[...] = (turned + extra[None]).astype(BF16)
            dzr[octave] = zmsg[z]
            along_z(lambda k: dz_copy(k).start())

    for j in range(4):
        side = (1 - xl) if j < 2 else xl
        cols = pl.ds(pl.multiple_of(side * 512 + half(j % 2) * 256, 256), 256)
        term = dot(normed_t[cols, :], dhid[...]).reshape(4, 2, 2, 16, HID)
        for bit in range(2):
            mine_t, other_t = term[:, bit, 0], term[:, bit, 1]
            own[j, bit] = jnp.where(low, mine_t, other_t)
            sib[j, bit] = jnp.where(low, other_t, mine_t).astype(BF16)
        co_copy(j).start()
        if j >= 1:
            near_send(j - 1)
        if j == 2:
            turn()

    near_send(3)

    def z_copy(k):
        ww = rem(w + k, NW)
        return copy(zs.at[ww], zb.at[w], s_z, r_z, dev(xl, 2 * ww + s_bit, c, f))

    zb[w] = jnp.zeros((16, HID), BF16)
    for h in range(2):
        kept = core_sum(2 + h, s_bit)
        for u in range(2):
            quarter = half(h) * 2 + u
            wait_from(xn.at[quarter], s_xm, r_xm.at[quarter])
            merged = kept[2 * u : 2 * u + 2] + xn[quarter].astype(F32)
            wait_from(xb.at[quarter], s_x, r_x.at[quarter])
            sides = [
                xb[quarter, n].astype(F32) + xb[quarter, 2 + n].astype(F32) for n in range(2)
            ]
            merged = merged + jnp.concatenate(sides, axis=2)
            blocks = pl.ds(quarter * 2, 2)
            totf[blocks] = merged
            zs[blocks] = merged.astype(BF16)
            for k in (4, 3, 5, 2, 6, 1, 7):

                @pl.when(div(rem(w + k, NW), 2) == quarter)
                def _():
                    z_copy(k).start()

    @pl.when(turning)
    def _():
        wait_from(dzr.at[1 - octave], s_dz, r_dz)

    @pl.when(jnp.logical_not(turning))
    def _():
        wait_from(dzr, s_dz, r_dz)

    pair = (dzr[0].astype(F32) + dzr[1].astype(F32)).astype(BF16)
    dzm[...] = pair
    dzf[f] = pair

    def df_copy(k):
        return copy(dzm, dzf.at[f], s_df, r_df, (d, fs[k]))

    for _, kf in near:
        df_copy(kf).start()

    def pc_copy():
        return copy(pall.at[c], pall.at[c], s_pc, r_pc, dev(xl, z, 1 - c, f))

    wait_from(pall.at[c, 0 : NZ - 1], s_pz, r_pz)
    pc_copy().start()

    wait_from(dzf.at[0 : NF - 1], s_df, r_df)
    wait_from(pall.at[1 - c], s_pc, r_pc)
    acc = jnp.zeros((16, HID), F32)
    loss = jnp.zeros((16, 128), F32)
    for g in range(NF):
        left = dzf[g]
        loss = loss + left.astype(F32)
        right = jnp.concatenate([pall[cc, zz] for zz in (g, g + NF) for cc in range(2)], axis=0)
        acc = acc + dot(left[:, :64], right)
    out_ref[16:32, :] = acc.astype(BF16)
    loss = jnp.sum(jnp.where(iota((16, 128), 1) >= 64, loss, 0.0), axis=1, keepdims=True)
    loss_ref[...] = jnp.broadcast_to(loss[:8], (8, 128)) * (1.0 / IMAGES)

    sent(tp.at[0:3], s_tq, r_tq)
    sent(tj.at[0 : NZ - 1], s_tz, r_tz)
    sent(c1b.at[0 : NF - 1], s_c1, r_c1)
    sent(px, s_px, r_px)
    sent(sj.at[0 : NZ - 1], s_cz, r_cz)
    sent(sp.at[0 : NP - 1], s_cp, r_cp)
    sent(da.at[0 : NP - 1], s_da, r_da)
    sent(pall.at[c, 0 : NZ - 1], s_pz, r_pz)
    sent(db.at[0 : (NF - 1) * 16], s_db.at[0], r_db.at[0])
    sent(db.at[0 : (NP - NF) * 16], s_db.at[1], r_db.at[1])
    sent(dzf.at[0 : NF - 1], s_df, r_df)

    @pl.when(turning)
    def _():
        sent(zmsg.at[0 : NZ - 1], s_dz, r_dz)

    sent(sib, s_co, r_co.at[0])
    sent(xs, s_x, r_x.at[0])
    sent(xm, s_xm, r_xm.at[0])
    sent(pall.at[c], s_pc, r_pc)

    wait_from(zb.at[0 : NW - 1], s_z, r_z)
    out_ref[0:16, :] = (totf[w] + jnp.sum(zb[...].astype(F32), axis=0)).astype(BF16)
    sent(zb.at[0 : NW - 1], s_z, r_z)


def body(tokens, teacher, norm_gain, w_in, b_in, w_out, b_out, final_gain):
    vmem = pl.BlockSpec(memory_space=pltpu.VMEM)
    one, two, four = (
        pltpu.SemaphoreType.DMA, pltpu.SemaphoreType.DMA((2,)), pltpu.SemaphoreType.DMA((4,))
    )
    sems = [one, one] * 7 + [two, two] + [one, one] * 4 + [one, four] + [one, four] * 2 + [one, one]
    packed, loss = pl.pallas_call(
        kernel,
        name="gram_step",
        out_shape=(
            jax.ShapeDtypeStruct((32, HID), BF16),
            jax.ShapeDtypeStruct((8, 128), F32),
        ),
        in_specs=[pl.BlockSpec(memory_space=pl.ANY)] * 8,
        out_specs=(vmem, vmem),
        scratch_shapes=[
            pltpu.VMEM((1024, D), BF16),
            pltpu.VMEM((8, DT), BF16),
            pltpu.VMEM((1, D), F32),
            pltpu.VMEM((D, HID), BF16),
            pltpu.VMEM((1, HID), F32),
            pltpu.VMEM((D, HID), BF16),
            pltpu.VMEM((8, 128), F32),
            pltpu.VMEM((8, 128), F32),
            pltpu.SemaphoreType.DMA((11,)),
            pltpu.VMEM((1024, D), BF16),
            pltpu.VMEM((D, 1024), BF16),
            pltpu.VMEM((1024, HID), F32),
            pltpu.VMEM((1024, HID), F32),
            pltpu.VMEM((1024, HID), BF16),
            pltpu.VMEM((8, D), F32),
            pltpu.VMEM((8, HID), F32),
            pltpu.VMEM((64, 128), F32),
            pltpu.VMEM((64, 128), F32),
            pltpu.VMEM((3, 128, 128), F32),
            pltpu.VMEM((4, 128, 384), BF16),
            pltpu.VMEM((NZ, 16, 384), BF16),
            pltpu.VMEM((16, 384), BF16),
            pltpu.VMEM((NF, 8, 128), F32),
            pltpu.VMEM((8, 128), F32),
            pltpu.VMEM((NP, 8, 128), F32),
            pltpu.VMEM((NZ, 8, 128), F32),
            pltpu.VMEM((NP, 8, 128), F32),
            pltpu.VMEM((NP, 8, 128), F32),
            pltpu.VMEM((16, 128), BF16),
            pltpu.VMEM((NP * 16, 128), BF16),
            pltpu.VMEM((NP * 16, 128), F32),
            pltpu.VMEM((8, HID), F32),
            pltpu.VMEM((8, HID), F32),
            pltpu.VMEM((16, HID), BF16),
            pltpu.VMEM((2, NZ, 16, HID), BF16),
            pltpu.VMEM((NZ, 16, 128), BF16),
            pltpu.VMEM((2, 16, 128), BF16),
            pltpu.VMEM((16, 128), BF16),
            pltpu.VMEM((NF, 16, 128), BF16),
            pltpu.VMEM((4, 2, 4, 16, HID), F32),
            pltpu.VMEM((4, 2, 4, 16, HID), BF16),
            pltpu.VMEM((4, 2, 4, 16, HID), BF16),
            pltpu.VMEM((4, 4, 2, 16, HID // 2), BF16),
            pltpu.VMEM((4, 4, 2, 16, HID // 2), BF16),
            pltpu.VMEM((4, 2, 16, HID), BF16),
            pltpu.VMEM((4, 2, 16, HID), BF16),
            pltpu.VMEM((NW, 16, HID), F32),
            pltpu.VMEM((NW, 16, HID), BF16),
            pltpu.VMEM((NW, 16, HID), BF16),
        ]
        + sems
        + [pltpu.SemaphoreType.REGULAR],
        compiler_params=pltpu.CompilerParams(
            collective_id=0, has_side_effects=True, vmem_limit_bytes=56 << 20
        ),
        cost_estimate=pl.CostEstimate(
            flops=5_000_000_000, bytes_accessed=8_000_000, transcendentals=1_000_000
        ),
    )(
        tokens,
        teacher,
        norm_gain.reshape(1, D),
        w_in,
        b_in.reshape(1, HID),
        w_out,
        b_out.reshape(8, 128),
        final_gain.reshape(8, 128),
    )
    return loss[0, 0], packed[:16], packed[16:]


def solution(mesh):
    return jax.shard_map(
        body,
        mesh=mesh,
        in_specs=(
            P("dp", None),
            P("dp", None),
            P(),
            P(None, "fsdp"),
            P("fsdp"),
            P(None, "fsdp"),
            P(),
            P(),
        ),
        out_specs=(P(), P("dp", "fsdp"), P("dp", "fsdp")),
        check_vma=False,
    )
```

```python
import jax
import jax.numpy as jnp
from jax import lax
from jax.experimental import pallas as pl
from jax.experimental.pallas import tpu as pltpu
from jax.sharding import PartitionSpec as P

MESH = pl.DeviceIdType.MESH
F32 = jnp.float32
BF16 = jnp.bfloat16

NZ = 16
NF = 8
NW = 8
NP = 32
LOSS_SCALE = 4096.0
IMAGES = 512
PER_IMAGE = 128
D = 1024
DT = 6144
HID = 512


def dot(left, right):
    return jnp.dot(left, right, preferred_element_type=F32)


def dot_last(left, right):
    return lax.dot_general(left, right, (((1,), (1,)), ((), ())), preferred_element_type=F32)


def dot_first(left, right):
    return lax.dot_general(left, right, (((0,), (0,)), ((), ())), preferred_element_type=F32)


def dot_exact(values, ones):
    high = values.astype(BF16)
    rest = values - high.astype(F32)
    mid = rest.astype(BF16)
    low = (rest - mid.astype(F32)).astype(BF16)
    return dot(high, ones) + dot(mid, ones) + dot(low, ones)


def div(value, by):
    return lax.div(value, jnp.int32(by))


def rem(value, by):
    return lax.rem(value, jnp.int32(by))


def iota(shape, axis):
    return lax.broadcasted_iota(jnp.int32, shape, axis)


def gelu_parts(values):
    inner = 0.7978845608 * (values + 0.044715 * values * values * values)
    return jnp.tanh(inner)


def kernel(
    tok_h, tea_h, ng_h, win_h, b_in_h, wout_h, b_out_h, fg_h,
    out_ref, loss_ref,
    tok, tea, ng, win, b_in, wout, b_out, fg, s_in,
    normed, normed_t, pre, slope, dhid, tmean, pooled_f, part64, tm64,
    tflat, tp, tj, trow, c1b, st_row, sp, sj, dref, da, dmsg, db, dbf,
    px, pin, pout16, pall, zmsg, dzr, dzm, dzf,
    own, sib, coreb, xs, xb, xm, xn, totf, zs, zb,
    s_tq, r_tq, s_tz, r_tz, s_c1, r_c1, s_px, r_px, s_cz, r_cz, s_cp, r_cp,
    s_da, r_da, s_db, r_db, s_pz, r_pz, s_pc, r_pc, s_dz, r_dz, s_df, r_df,
    s_co, r_co, s_x, r_x, s_xm, r_xm, s_z, r_z, s_far,
):
    d = lax.axis_index("dp")
    f = lax.axis_index("fsdp")
    xl = div(d, 2 * NZ)
    z = rem(div(d, 2), NZ)
    c = rem(d, 2)
    q = xl * 2 + c
    p = q * NF + f

    def dev(xx, zz, cc, ff):
        return ((xx * NZ + zz) * 2 + cc, ff)

    qs = [rem(q + k, 4) for k in range(4)]
    fs = [rem(f + k, NF) for k in range(NF)]
    ds = [(div(v, 2) * NZ + z) * 2 + rem(v, 2) for v in qs]
    near = [(0, kf) for kf in (3, 5, 4, 7, 1, 6, 2)]
    others = [(kq, kf) for kq in (2, 3, 1) for kf in (3, 5, 4, 7, 1, 6, 2, 0)]
    plane = near + others
    far_z = [NZ // 2 + (m + 1) // 2 * (1 - 2 * (m % 2)) for m in range(NZ - 1)]
    step_z = NZ // 4
    close_z = [k for k in far_z if min(k, NZ - k) <= step_z]
    away_z = [k for k in far_z if k not in close_z]

    def copy(src, dst, ss, rs, to):
        return pltpu.make_async_remote_copy(
            src_ref=src, dst_ref=dst, send_sem=ss, recv_sem=rs, device_id=to, device_id_type=MESH
        )

    def each(lo, hi, fn):
        def step(k, carry):
            fn(k)
            return carry

        lax.fori_loop(lo, hi, step, 0)

    def along_z(fn, steps=far_z):
        for k in steps:
            fn(k)

    def load(n, src, dst):
        return pltpu.make_async_copy(src, dst, s_in.at[n])

    def load_tok(i):
        rows = pl.ds(pl.multiple_of(i * 256, 256), 256)
        return load(i, tok_h.at[rows], tok.at[rows])

    loads = [
        load(4 + n, src, dst)
        for n, (src, dst) in enumerate(
            [
                (tea_h, tea), (ng_h, ng), (win_h, win), (b_in_h, b_in),
                (wout_h, wout), (b_out_h, b_out), (fg_h, fg),
            ]
        )
    ]
    loads[0].start()
    loads[1].start()
    load_tok(0).start()
    loads[2].start()
    loads[3].start()
    each(1, 4, lambda i: load_tok(i).start())
    for item in loads[4:]:
        item.start()

    barrier = pltpu.get_barrier_semaphore()

    for k in close_z:
        pl.semaphore_signal(
            barrier, inc=1, device_id=dev(xl, rem(z + k, NZ), c, f), device_id_type=MESH
        )
    for kq, kf in plane:
        pl.semaphore_signal(barrier, inc=1, device_id=(ds[kq], fs[kf]), device_id_type=MESH)

    loads[0].wait()
    teacher = tea[...].astype(F32)
    t_norm = jnp.sqrt(jnp.sum(teacher * teacher, axis=-1, keepdims=True) + 1e-06)
    target = teacher / t_norm
    for a in range(16):
        for b in range(3):
            lo = 384 * a + 128 * b
            tflat[b, pl.ds(a, 8, stride=16), :] = target[:, lo : lo + 128]
    tp[q] = jnp.concatenate([tflat[b] for b in range(3)], axis=1).astype(BF16)
    own_rows = pl.ds(pl.multiple_of(f * 16, 16), 16)
    own_target = jnp.concatenate([tflat[b, own_rows, :] for b in range(3)], axis=1).astype(BF16)
    trow[...] = own_target
    tj[z] = own_target

    for item in loads[1:4]:
        item.wait()
    gain = ng[...]
    bias = b_in[...]

    def normalise(i):
        rows = slice(256 * i, 256 * i + 256)
        x = tok[rows, :].astype(F32)
        for n in range(2):
            tmean[2 * i + n : 2 * i + n + 1, :] = jnp.sum(
                x[128 * n : 128 * n + 128], axis=0, keepdims=True
            ) * (1.0 / PER_IMAGE)
        centered = x - jnp.mean(x, axis=-1, keepdims=True)
        inv = lax.rsqrt(jnp.mean(centered * centered, axis=-1, keepdims=True) + 1e-05)
        normed[rows, :] = (centered * inv * gain).astype(BF16)

    def activate(i):
        rows = slice(256 * i, 256 * i + 256)
        act = dot(normed[rows, :], win[...]) + bias
        pre[rows, :] = act
        g = 0.5 * act * (1.0 + gelu_parts(act))
        for n in range(2):
            pooled_f[2 * i + n : 2 * i + n + 1, :] = jnp.sum(
                g[128 * n : 128 * n + 128], axis=0, keepdims=True
            ) * (1.0 / PER_IMAGE)

    load_tok(0).wait()
    normalise(0)
    for i in range(2):
        load_tok(i + 1).wait()
        activate(i)
        normalise(i + 1)
    def tz_copy(k):
        return copy(trow, tj.at[z], s_tz, r_tz, dev(xl, rem(z + k, NZ), c, f))

    pl.semaphore_wait(barrier, NP - 1 + len(close_z))
    for k in (step_z, NZ - step_z):
        pl.semaphore_signal(
            s_far, inc=1, device_id=dev(xl, rem(z + k, NZ), c, f), device_id_type=MESH
        )
    along_z(lambda k: tz_copy(k).start(), close_z)

    load_tok(3).wait()
    activate(2)
    normalise(3)
    activate(3)
    for item in loads[4:]:
        item.wait()
    pooled_b = pooled_f[...].astype(BF16)
    partial = dot_last(pooled_b, wout[...])
    mean_tok = tmean[...]
    for a in range(8):
        part64[pl.ds(a, 8, stride=8), :] = partial[:, 128 * a : 128 * a + 128]
        tm64[pl.ds(a, 8, stride=8), :] = mean_tok[:, 128 * a : 128 * a + 128]

    def c1_copy(k):
        ff = rem(f + k, NF)
        return copy(
            part64.at[pl.ds(pl.multiple_of(ff * 8, 8), 8)],
            c1b.at[f], s_c1, r_c1, (d, ff),
        )

    def tq_copy(k):
        qq = rem(q + k, 4)
        return copy(
            tp.at[q], tp.at[q], s_tq, r_tq, dev(div(qq, 2), z, rem(qq, 2), f)
        )


    for _, kf in near:
        c1_copy(kf).start()
    c1b[f] = part64[pl.ds(pl.multiple_of(f * 8, 8), 8), :]
    px[...] = pooled_b.astype(F32)

    def px_copy():
        return copy(px, pin, s_px, r_px, dev(1 - xl, z, c, f))

    px_copy().start()

    def slopes(i):
        rows = pl.ds(pl.multiple_of(i * 128, 128), 128)
        v = pre[rows, :]
        t = gelu_parts(v)
        slope[rows, :] = 0.5 * (1.0 + t) + 0.5 * v * (1.0 - t * t) * 0.7978845608 * (
            1.0 + 3.0 * 0.044715 * v * v
        )

    each(0, 8, slopes)

    def wait_from(dst, ss, rs):
        copy(dst, dst, ss, rs, (d, f)).wait_recv()

    def sent(src, ss, rs):
        copy(src, src, ss, rs, (d, f)).wait_send()

    pl.semaphore_wait(s_far, 2)
    along_z(lambda k: tz_copy(k).start(), away_z)

    wait_from(c1b.at[0 : NF - 1], s_c1, r_c1)
    embedding = jnp.sum(c1b[...], axis=0) + tm64[pl.ds(pl.multiple_of(f * 8, 8), 8), :] + b_out[...]
    final_gain = fg[...]

    def total(v):
        return jnp.sum(jnp.sum(v, axis=1, keepdims=True), axis=0, keepdims=True)

    cent = embedding - total(embedding) * (1.0 / D)
    inv_std = lax.rsqrt(total(cent * cent) * (1.0 / D) + 1e-05)
    n_emb = cent * inv_std
    unit = n_emb * final_gain
    unit_norm = jnp.sqrt(total(unit * unit) + 1e-06)
    unit_dir = unit / unit_norm
    student = unit_dir.astype(BF16).astype(F32)
    st_row[...] = student

    def cz_copy(k):
        return copy(st_row, sj.at[z], s_cz, r_cz, dev(xl, rem(z + k, NZ), c, f))

    def cp_copy(k):
        return copy(st_row, sp.at[p], s_cp, r_cp, (ds[k[0]], fs[k[1]]))

    along_z(lambda k: cz_copy(k).start())
    for k in plane:
        cp_copy(k).start()
    each(1, 4, lambda k: tq_copy(k).start())
    sj[z] = student
    sp[p] = student

    for i in range(4):
        turned_cols = slice(256 * i, 256 * i + 256)
        normed_t[turned_cols, :] = normed[:, turned_cols].T

    wait_from(tp.at[0:3], s_tq, r_tq)
    wait_from(tj.at[0 : NZ - 1], s_tz, r_tz)
    tx = dot_last(tp[...].reshape(NP * 16, 384), tj[...].reshape(NZ * 16, 384))
    same = (iota(tx.shape, 0) % 16) == (iota(tx.shape, 1) % 16)
    tx = jnp.sum(jnp.where(same, tx, 0.0).reshape(NP, 16, NZ * 16), axis=1)
    spread = ((iota((NZ * 16, 128), 0) // 16) == (iota((NZ * 16, 128), 1) // 8)).astype(BF16)
    gram_t = dot_exact(tx, spread)

    def pz_copy(k):
        return copy(
            pout16, pall.at[c, z], s_pz, r_pz, dev(xl, rem(z + k, NZ), c, f)
        )

    wait_from(pin, s_px, r_px)
    mine, other = px[...], pin[...]
    first = xl == 0
    block16 = jnp.concatenate(
        [jnp.where(first, mine, other), jnp.where(first, other, mine)], axis=0
    ).astype(BF16)
    pout16[...] = block16
    pall[c, z] = block16

    wait_from(sp.at[0 : NP - 1], s_cp, r_cp)
    wait_from(sj.at[0 : NZ - 1], s_cz, r_cz)
    s_plane = sp[...].reshape(NP * 8, 128).astype(BF16)
    s_other = sj[...].reshape(NZ * 8, 128).astype(BF16)
    sx = dot_last(s_plane, s_other)
    diag = (iota(sx.shape, 0) % 8) == (iota(sx.shape, 1) % 8)
    sx = jnp.sum(jnp.where(diag, sx, 0.0).reshape(NP, 8, 128), axis=1)
    group = ((iota((128, 128), 0) // 8) == (iota((128, 128), 1) // 8)).astype(BF16)
    resid = dot_exact(sx, group) - gram_t
    share = total(resid * resid) * 0.125
    wide = jnp.broadcast_to(resid[:, None, :], (NP, 8, 128)).reshape(NP * 8, 128)
    wide = jnp.where(diag, wide, 0.0).astype(BF16)
    dref[...] = dot(wide, s_other).reshape(NP, 8, 128)

    def da_copy(k):
        return copy(
            dref.at[qs[k[0]] * NF + fs[k[1]]], da.at[p], s_da, r_da, (ds[k[0]], fs[k[1]])
        )

    for k in plane:
        da_copy(k).start()
    da[p] = dref[p]
    along_z(lambda k: pz_copy(k).start(), away_z)

    wait_from(da.at[0 : NP - 1], s_da, r_da)
    dstudent = (LOSS_SCALE * 4.0 / IMAGES) * jnp.sum(da[...], axis=0)
    dunit = (dstudent - unit_dir * total(unit_dir * dstudent)) / unit_norm
    gain_grad = dunit * final_gain
    dembed = inv_std * (
        gain_grad - total(gain_grad) * (1.0 / D) - n_emb * (total(gain_grad * n_emb) * (1.0 / D))
    )
    high = share.astype(BF16).astype(F32)
    mid = (share - high).astype(BF16).astype(F32)
    last = share - high - mid
    row = iota((8, 128), 0)
    terms = jnp.where(row == 0, high, jnp.where(row == 1, mid, jnp.where(row == 2, last, 0.0)))
    message = jnp.concatenate([dembed, terms], axis=0).astype(BF16)
    dmsg[...] = message

    def rows16(pp):
        return pl.ds(pl.multiple_of(pp * 16, 16), 16)

    def db_copy(k, part):
        return copy(
            dmsg, db.at[rows16(p)], s_db.at[part], r_db.at[part], (ds[k[0]], fs[k[1]])
        )

    for k in near:
        db_copy(k, 0).start()
    for k in others:
        db_copy(k, 1).start()
    along_z(lambda k: pz_copy(k).start(), close_z)
    db[rows16(p), :] = message

    wait_from(db.at[0 : (NF - 1) * 16], s_db.at[0], r_db.at[0])
    own_rows = pl.ds(pl.multiple_of(q * (NF * 16), NF * 16), NF * 16)
    dbf[own_rows, :] = db[own_rows, :].astype(F32)
    block = jnp.concatenate(
        [dbf[pl.ds(q * (NF * 16) + a, 8, stride=16), :] for a in range(8)], axis=1
    ).astype(BF16)
    tmean[:, :HID] = dot(block, wout[...]) * (1.0 / PER_IMAGE)

    def hidden(i):
        rows = pl.ds(pl.multiple_of(i * PER_IMAGE, PER_IMAGE), PER_IMAGE)
        dhid[rows, :] = (tmean[pl.ds(i, 1), :HID] * slope[rows, :]).astype(BF16)

    each(0, 8, hidden)

    low = c == 0
    s_bit = rem(z, 2)
    w = div(z, 2)

    def half(h):
        return rem(div(w, 4) + 1 + h, 2)

    def co_copy(j):
        return copy(sib.at[j], coreb.at[j], s_co, r_co.at[j], dev(xl, z, 1 - c, f))

    step = 1 - 2 * s_bit

    def near_copy(t, quarter):
        xx = xl if t >= 3 else 1 - xl
        zz = z if t == 2 else rem(z + NZ + (step if t in (0, 3) else -step), NZ)
        to = dev(xx, zz, c, f)
        if t == 2:
            return copy(xm.at[quarter], xn.at[quarter], s_xm, r_xm.at[quarter], to)
        n = t if t < 2 else t - 1
        return copy(xs.at[n, quarter], xb.at[quarter, n], s_x, r_x.at[quarter], to)

    def part(h, u):
        return rem(div(rem(w, 4), 2) + h + u, 2)

    def core_sum(j, bit, u):
        two = pl.ds(2 * part(j % 2, u), 2)
        return own[j, bit, two] + coreb[j, bit, two].astype(F32)

    def near_send(j):
        wait_from(coreb.at[j], s_co, r_co.at[j])
        for u in range(2):
            quarter = half(j % 2) * 2 + part(j % 2, u)
            across = core_sum(j, 1 - s_bit, u).astype(BF16)
            for n in range(2):
                t = n if j < 2 else 3 + n
                xs[t - t // 3, quarter] = across[:, :, 256 * n : 256 * n + 256]
                near_copy(t, quarter).start()
            if j < 2:
                xm[quarter] = core_sum(j, s_bit, u).astype(BF16)
                near_copy(2, quarter).start()

    octave = div(z, NF)
    turning = rem(z, NF) == f

    def dz_copy(k):
        zz = rem(z + k, NZ)
        return copy(zmsg.at[zz], dzr.at[octave], s_dz, r_dz, dev(xl, zz, c, f))

    def turn():
        wait_from(db.at[0 : (NP - NF) * 16], s_db.at[1], r_db.at[1])

        @pl.when(turning)
        def _():
            dbf[...] = db[...].astype(F32)
            loss_plane = jnp.zeros((8, 128), F32)
            for pp in range(NP):
                loss_plane = loss_plane + dbf[pp * 16 + 8 : pp * 16 + 16, :]
            loss_plane = jnp.sum(loss_plane, axis=0, keepdims=True)
            flat = jnp.concatenate(
                [dbf[pl.ds(xl * 4 + a, NP, stride=16), :] for a in range(4)], axis=1
            ).astype(BF16)
            image = iota((NP, 128), 0)
            lane = octave * 32 + ((image // 8) % 2) * 16 + (image // 16) * 8 + image % 8
            place = (lane == iota((NP, 128), 1)).astype(BF16)
            turned = dot_first(flat, place).reshape(NZ, 2, 16, 128)
            turned = jnp.where(low, turned[:, 0], turned[:, 1])
            high = loss_plane.astype(BF16).astype(F32)
            mid = (loss_plane - high).astype(BF16).astype(F32)
            last = loss_plane - high - mid
            at = iota((1, 128), 1) - (64 + 4 * octave)
            extra = jnp.where(
                at == 0, high, jnp.where(at == 1, mid, jnp.where(at == 2, last, 0.0))
            )
            zmsg[...] = (turned + extra[None]).astype(BF16)
            dzr[octave] = zmsg[z]
            along_z(lambda k: dz_copy(k).start())

    for j in range(4):
        side = (1 - xl) if j < 2 else xl
        cols = pl.ds(pl.multiple_of(side * 512 + half(j % 2) * 256, 256), 256)
        term = dot(normed_t[cols, :], dhid[...]).reshape(4, 2, 2, 16, HID)
        for bit in range(2):
            mine_t, other_t = term[:, bit, 0], term[:, bit, 1]
            own[j, bit] = jnp.where(low, mine_t, other_t)
            sib[j, bit] = jnp.where(low, other_t, mine_t).astype(BF16)
        co_copy(j).start()
        if j >= 1:
            near_send(j - 1)
        if j == 2:
            turn()

    near_send(3)

    def z_copy(k):
        ww = rem(w + k, NW)
        return copy(zs.at[ww], zb.at[w], s_z, r_z, dev(xl, 2 * ww + s_bit, c, f))

    zb[w] = jnp.zeros((16, HID), BF16)
    for h in range(2):
        for u in range(2):
            quarter = half(h) * 2 + part(h, u)
            wait_from(xn.at[quarter], s_xm, r_xm.at[quarter])
            merged = core_sum(2 + h, s_bit, u) + xn[quarter].astype(F32)
            wait_from(xb.at[quarter], s_x, r_x.at[quarter])
            sides = [
                xb[quarter, n].astype(F32) + xb[quarter, 2 + n].astype(F32) for n in range(2)
            ]
            merged = merged + jnp.concatenate(sides, axis=2)
            blocks = pl.ds(quarter * 2, 2)
            totf[blocks] = merged
            zs[blocks] = merged.astype(BF16)
            for k in (4, 3, 5, 2, 6, 1, 7):

                @pl.when(div(rem(w + k, NW), 2) == quarter)
                def _():
                    z_copy(k).start()

    @pl.when(turning)
    def _():
        wait_from(dzr.at[1 - octave], s_dz, r_dz)

    @pl.when(jnp.logical_not(turning))
    def _():
        wait_from(dzr, s_dz, r_dz)

    pair = (dzr[0].astype(F32) + dzr[1].astype(F32)).astype(BF16)
    dzm[...] = pair
    dzf[f] = pair

    def df_copy(k):
        return copy(dzm, dzf.at[f], s_df, r_df, (d, fs[k]))

    for _, kf in near:
        df_copy(kf).start()

    def pc_copy():
        return copy(pall.at[c], pall.at[c], s_pc, r_pc, dev(xl, z, 1 - c, f))

    wait_from(pall.at[c, 0 : NZ - 1], s_pz, r_pz)
    pc_copy().start()

    wait_from(dzf.at[0 : NF - 1], s_df, r_df)
    wait_from(pall.at[1 - c], s_pc, r_pc)
    acc = jnp.zeros((16, HID), F32)
    loss = jnp.zeros((16, 128), F32)
    for g in range(NF):
        left = dzf[g]
        loss = loss + left.astype(F32)
        right = jnp.concatenate([pall[cc, zz] for zz in (g, g + NF) for cc in range(2)], axis=0)
        acc = acc + dot(left[:, :64], right)
    out_ref[16:32, :] = acc.astype(BF16)
    loss = jnp.sum(jnp.where(iota((16, 128), 1) >= 64, loss, 0.0), axis=1, keepdims=True)
    loss_ref[...] = jnp.broadcast_to(loss[:8], (8, 128)) * (1.0 / IMAGES)

    sent(tp.at[0:3], s_tq, r_tq)
    sent(tj.at[0 : NZ - 1], s_tz, r_tz)
    sent(c1b.at[0 : NF - 1], s_c1, r_c1)
    sent(px, s_px, r_px)
    sent(sj.at[0 : NZ - 1], s_cz, r_cz)
    sent(sp.at[0 : NP - 1], s_cp, r_cp)
    sent(da.at[0 : NP - 1], s_da, r_da)
    sent(pall.at[c, 0 : NZ - 1], s_pz, r_pz)
    sent(db.at[0 : (NF - 1) * 16], s_db.at[0], r_db.at[0])
    sent(db.at[0 : (NP - NF) * 16], s_db.at[1], r_db.at[1])
    sent(dzf.at[0 : NF - 1], s_df, r_df)

    @pl.when(turning)
    def _():
        sent(zmsg.at[0 : NZ - 1], s_dz, r_dz)

    sent(sib, s_co, r_co.at[0])
    sent(xs, s_x, r_x.at[0])
    sent(xm, s_xm, r_xm.at[0])
    sent(pall.at[c], s_pc, r_pc)

    wait_from(zb.at[0 : NW - 1], s_z, r_z)
    out_ref[0:16, :] = (totf[w] + jnp.sum(zb[...].astype(F32), axis=0)).astype(BF16)
    sent(zb.at[0 : NW - 1], s_z, r_z)


def body(tokens, teacher, norm_gain, w_in, b_in, w_out, b_out, final_gain):
    vmem = pl.BlockSpec(memory_space=pltpu.VMEM)
    one, two, four = (
        pltpu.SemaphoreType.DMA, pltpu.SemaphoreType.DMA((2,)), pltpu.SemaphoreType.DMA((4,))
    )
    sems = [one, one] * 7 + [two, two] + [one, one] * 4 + [one, four] + [one, four] * 2 + [one, one]
    packed, loss = pl.pallas_call(
        kernel,
        name="gram_step",
        out_shape=(
            jax.ShapeDtypeStruct((32, HID), BF16),
            jax.ShapeDtypeStruct((8, 128), F32),
        ),
        in_specs=[pl.BlockSpec(memory_space=pl.ANY)] * 8,
        out_specs=(vmem, vmem),
        scratch_shapes=[
            pltpu.VMEM((1024, D), BF16),
            pltpu.VMEM((8, DT), BF16),
            pltpu.VMEM((1, D), F32),
            pltpu.VMEM((D, HID), BF16),
            pltpu.VMEM((1, HID), F32),
            pltpu.VMEM((D, HID), BF16),
            pltpu.VMEM((8, 128), F32),
            pltpu.VMEM((8, 128), F32),
            pltpu.SemaphoreType.DMA((11,)),
            pltpu.VMEM((1024, D), BF16),
            pltpu.VMEM((D, 1024), BF16),
            pltpu.VMEM((1024, HID), F32),
            pltpu.VMEM((1024, HID), F32),
            pltpu.VMEM((1024, HID), BF16),
            pltpu.VMEM((8, D), F32),
            pltpu.VMEM((8, HID), F32),
            pltpu.VMEM((64, 128), F32),
            pltpu.VMEM((64, 128), F32),
            pltpu.VMEM((3, 128, 128), F32),
            pltpu.VMEM((4, 128, 384), BF16),
            pltpu.VMEM((NZ, 16, 384), BF16),
            pltpu.VMEM((16, 384), BF16),
            pltpu.VMEM((NF, 8, 128), F32),
            pltpu.VMEM((8, 128), F32),
            pltpu.VMEM((NP, 8, 128), F32),
            pltpu.VMEM((NZ, 8, 128), F32),
            pltpu.VMEM((NP, 8, 128), F32),
            pltpu.VMEM((NP, 8, 128), F32),
            pltpu.VMEM((16, 128), BF16),
            pltpu.VMEM((NP * 16, 128), BF16),
            pltpu.VMEM((NP * 16, 128), F32),
            pltpu.VMEM((8, HID), F32),
            pltpu.VMEM((8, HID), F32),
            pltpu.VMEM((16, HID), BF16),
            pltpu.VMEM((2, NZ, 16, HID), BF16),
            pltpu.VMEM((NZ, 16, 128), BF16),
            pltpu.VMEM((2, 16, 128), BF16),
            pltpu.VMEM((16, 128), BF16),
            pltpu.VMEM((NF, 16, 128), BF16),
            pltpu.VMEM((4, 2, 4, 16, HID), F32),
            pltpu.VMEM((4, 2, 4, 16, HID), BF16),
            pltpu.VMEM((4, 2, 4, 16, HID), BF16),
            pltpu.VMEM((4, 4, 2, 16, HID // 2), BF16),
            pltpu.VMEM((4, 4, 2, 16, HID // 2), BF16),
            pltpu.VMEM((4, 2, 16, HID), BF16),
            pltpu.VMEM((4, 2, 16, HID), BF16),
            pltpu.VMEM((NW, 16, HID), F32),
            pltpu.VMEM((NW, 16, HID), BF16),
            pltpu.VMEM((NW, 16, HID), BF16),
        ]
        + sems
        + [pltpu.SemaphoreType.REGULAR],
        compiler_params=pltpu.CompilerParams(
            collective_id=0, has_side_effects=True, vmem_limit_bytes=56 << 20
        ),
        cost_estimate=pl.CostEstimate(
            flops=5_000_000_000, bytes_accessed=8_000_000, transcendentals=1_000_000
        ),
    )(
        tokens,
        teacher,
        norm_gain.reshape(1, D),
        w_in,
        b_in.reshape(1, HID),
        w_out,
        b_out.reshape(8, 128),
        final_gain.reshape(8, 128),
    )
    return loss[0, 0], packed[:16], packed[16:]


def solution(mesh):
    return jax.shard_map(
        body,
        mesh=mesh,
        in_specs=(
            P("dp", None),
            P("dp", None),
            P(),
            P(None, "fsdp"),
            P("fsdp"),
            P(None, "fsdp"),
            P(),
            P(),
        ),
        out_specs=(P(), P("dp", "fsdp"), P("dp", "fsdp")),
        check_vma=False,
    )
```
